128 devices in a mesh: gx: 16 (over z, y), gy: 8 (over x, core).
Axes of the slice: x: 4, y: 4, z: 4, core: 2. Of those that a mesh axis runs over, the one named last changes fastest.
Arguments:
- activations: bfloat16 [128, 16, 8192], P('gy', None, 'gx'), may hold values from -80 to 80
- norm_gain: bfloat16 [8192], P('gx'), may hold values from 0.099609375 to 1.8984375
- query_weight: bfloat16 [8192, 8192], P('gx', 'gy'), may hold values from -0.0625 to 0.0625
- key_weight: bfloat16 [8192, 1024], P('gx', 'gy'), may hold values from -0.0625 to 0.0625
- value_weight: bfloat16 [8192, 1024], P('gx', 'gy'), may hold values from -0.0625 to 0.0625
- out_weight: bfloat16 [8192, 8192], P('gy', 'gx'), may hold values from -0.0625 to 0.0625
- key_cache: bfloat16 [128, 4096, 1024], P(('gx', 'gy')), may hold values from -250 to 250
- value_cache: bfloat16 [128, 4096, 1024], P(('gx', 'gy')), may hold values from -16 to 16
- lengths: int32 [128], P(('gx', 'gy')), may hold values from 1 to 4096, as said below
- positions: int32 [128], P(('gx', 'gy')), may hold values from 0 to 8191
Outputs:
- mixed: bfloat16 [128, 16, 8192], P('gy', None, 'gx')
The draws below stay inside these ranges and needn't reach their ends.
Inputs may be any that keep to these rules, and one draw needn't show every extreme that they name: `lengths`: some sequence has length 1 and some has length 4096 in every draw.
All inputs are finite; a program needn't handle non-finite values.
Results may differ from the reference program's by a relative error of at most 0.019.
The reference program's roundings to bfloat16 on the way count: a program that leaves them out, or rounds other values in their place, can miss the bound.
Values may be sent and summed in bfloat16 or wider, within the bound.
A program may use at most 192 MiB of HBM per device.

```python
import math
import jax
import jax.numpy as jnp
from jax import lax

D = 8192
HEADS = 64
KV = 8
HD = 128
CTX = 4096
DRAFT = 16
BATCH = 128


def draw_activations(key, part):
    key = jax.random.fold_in(key, 3)
    first_key, second_key = jax.random.split(key, 2)
    ramp = 0.6 * jnp.exp(jnp.arange(D, dtype=jnp.float32) * (math.log(3.0) / (D - 1)))
    row_scale = jnp.exp(jax.random.uniform(second_key, (BATCH, DRAFT, 1)) * math.log(10.0))
    base = jnp.clip(jax.random.normal(first_key, (BATCH, DRAFT, D)), -4.0, 4.0)
    return jnp.clip(base * ramp * row_scale, -80.0, 80.0).astype(jnp.bfloat16)


def draw_key_cache(key, part):
    key = jax.random.fold_in(key, 5)
    first_key = jax.random.fold_in(key, 0)
    base = jnp.clip(jax.random.normal(first_key, (BATCH, CTX, KV, HD)), -4.0, 4.0)
    keys = 2.0 * base
    return keys.reshape(BATCH, CTX, KV * HD).astype(jnp.bfloat16)


def draw_lengths(key, part):
    key = jax.random.fold_in(key, 7)
    first_key, second_key, third_key = jax.random.split(key, 3)
    left = jax.random.randint(first_key, (BATCH,), 1, 65)
    right = jax.random.randint(second_key, (BATCH,), 1, 65)
    values = jnp.maximum(left * right * CTX // 4096, 1)
    picked = jax.random.permutation(third_key, BATCH)
    values = values.at[picked[0]].set(CTX)
    values = values.at[picked[1]].set(1)
    return values.astype(jnp.int32)


def place_ends(values, key, smallest, largest):
    index_at = [jax.random.randint(jax.random.fold_in(key, axis), (), 0, length) for axis, length in enumerate(values.shape)]
    widest = values.shape.index(max(values.shape))
    neighbour = index_at[:widest] + [(index_at[widest] + 1) % values.shape[widest]] + index_at[widest + 1:]
    return values.at[tuple(index_at)].set(smallest).at[tuple(neighbour)].set(largest)


def shard_levels(key, shape, pieces, smallest, high):
    def one(dim, shards_of):
        heights = jax.random.uniform(jax.random.fold_in(jax.random.fold_in(key, 6), dim), (shards_of,), jnp.float32, smallest / len(pieces), high / len(pieces))
        return jnp.repeat(jnp.exp(heights), shape[dim] // shards_of).reshape((-1,) + (1,) * (len(shape) - dim - 1))

    factor_of = one(*pieces[0])
    for cut in pieces[1:]:
        factor_of = factor_of * one(*cut)
    return factor_of


def bell_draw(rng, extent, width, bound, cuts=(), kind=jnp.bfloat16):
    gain = shard_levels(rng, extent, cuts, -0.22, 0.18) if cuts else 1.0
    array = jax.random.normal(rng, extent, jnp.float32) * width * gain
    return jnp.minimum(jnp.maximum(array, -bound), bound).astype(kind)


def setup_inputs(seed: int = 0) -> dict:
    splits = jax.random.split(jax.random.key(seed), 11)
    activations = draw_activations(jax.random.fold_in(splits[10], 71), 0)
    norm_gain = jnp.clip(1.0 + 0.18 * jax.random.normal(splits[1], (D,), jnp.float32), 0.099609375, 1.8984375).astype(jnp.bfloat16)
    query_weight = bell_draw(splits[2], (D, HEADS * HD), D ** -0.5, 0.0625, ((0, 16), (1, 8)))
    key_weight = bell_draw(splits[3], (D, KV * HD), D ** -0.5, 0.0625, ((0, 16), (1, 8)))
    value_weight = bell_draw(splits[4], (D, KV * HD), D ** -0.5, 0.0625, ((0, 16), (1, 8)))
    out_weight = bell_draw(splits[5], (HEADS * HD, D), (HEADS * HD) ** -0.5, 0.0625, ((0, 8), (1, 16)))
    key_cache = draw_key_cache(jax.random.fold_in(splits[10], 71), 0)
    value_cache = bell_draw(splits[7], (BATCH, CTX, KV * HD), 4.0, 16.0, ((0, 128),))
    lengths = draw_lengths(jax.random.fold_in(splits[10], 71), 0)
    positions = place_ends(jax.random.randint(splits[9], (BATCH,), 0, 8192), jax.random.fold_in(splits[9], 1), 0, 8191).astype(jnp.int32)
    return {"activations": activations, "norm_gain": norm_gain, "query_weight": query_weight, "key_weight": key_weight, "value_weight": value_weight, "out_weight": out_weight, "key_cache": key_cache, "value_cache": value_cache, "lengths": lengths, "positions": positions}


def rotate(vector, places):
    halfway = vector.shape[-1] // 2
    frequency = jnp.exp(jnp.arange(halfway, dtype=jnp.float32) * (-2.0 * math.log(500000.0) / vector.shape[-1]))
    angles = places.astype(jnp.float32)[..., None] * frequency
    cosine = jnp.cos(angles)[..., None, :]
    sine_part = jnp.sin(angles)[..., None, :]
    first_half = vector[..., :halfway]
    second = vector[..., halfway:]
    return jnp.concatenate([first_half * cosine - second * sine_part, second * cosine + first_half * sine_part], axis=-1)

def attend_row(query, fresh_keys, fresh_values, cache_keys, cache_values, length):
    drafts = query.shape[0]
    slots = cache_keys.shape[0]
    group_size = HEADS // KV
    query_heads = query.astype(jnp.float32).reshape(drafts, KV, group_size, HD)
    keys_old = cache_keys.astype(jnp.float32).reshape(slots, KV, HD)
    values_old = cache_values.astype(jnp.float32).reshape(slots, KV, HD)
    keys_new = fresh_keys.astype(jnp.float32).reshape(drafts, KV, HD)
    values_new = fresh_values.astype(jnp.float32).reshape(drafts, KV, HD)
    scaling = HD ** (-0.5)
    cached_scores = jnp.einsum('tkgd,ckd->kgtc', query_heads, keys_old) * scaling
    fresh_scores = jnp.einsum('tkgd,skd->kgts', query_heads, keys_new) * scaling
    visible = jnp.arange(slots, dtype=jnp.int32) < length
    causal = jnp.arange(drafts, dtype=jnp.int32)[None, :] <= jnp.arange(drafts, dtype=jnp.int32)[:, None]
    highest = jnp.maximum(lax.optimization_barrier(jnp.max(jnp.where(visible, cached_scores, -1e+30), axis=-1)), lax.optimization_barrier(jnp.max(jnp.where(causal, fresh_scores, -1e+30), axis=-1)))
    cached_weights = jnp.where(visible, jnp.exp(cached_scores - highest[..., None]), 0.0)
    fresh_weights = jnp.where(causal, jnp.exp(fresh_scores - highest[..., None]), 0.0)
    totals = lax.optimization_barrier(jnp.sum(cached_weights, axis=-1)) + lax.optimization_barrier(jnp.sum(fresh_weights, axis=-1))
    cached_bf = lax.optimization_barrier(cached_weights.astype(jnp.bfloat16)).astype(jnp.float32)
    fresh_bf = lax.optimization_barrier(fresh_weights.astype(jnp.bfloat16)).astype(jnp.float32)
    blended = jnp.einsum('kgtc,ckd->tkgd', cached_bf, values_old) + jnp.einsum('kgts,skd->tkgd', fresh_bf, values_new)
    result = blended / jnp.transpose(totals, (2, 0, 1))[..., None]
    return result.reshape(drafts, HEADS * HD).astype(jnp.bfloat16)

def reference(activations, norm_gain, query_weight, key_weight, value_weight, out_weight, key_cache, value_cache, lengths, positions):
    widened = activations.astype(jnp.float32)
    squares = lax.optimization_barrier(jnp.sum(widened * widened, axis=-1))
    rms_inv = lax.rsqrt(squares / D + 1e-05)
    scaled = (widened * norm_gain.astype(jnp.float32)).astype(jnp.bfloat16)
    flattened = scaled.reshape(BATCH * DRAFT, D)

    def project(weight):
        product = jnp.dot(flattened, weight, preferred_element_type=jnp.float32)
        return product.reshape(BATCH, DRAFT, weight.shape[1]) * rms_inv[..., None]
    places = positions[:, None] + jnp.arange(DRAFT, dtype=jnp.int32)[None, :]
    query_rot = rotate(project(query_weight).reshape(BATCH, DRAFT, HEADS, HD), places)
    query_rot = query_rot.reshape(BATCH, DRAFT, HEADS * HD).astype(jnp.bfloat16)
    key_rot = rotate(project(key_weight).reshape(BATCH, DRAFT, KV, HD), places)
    key_rot = key_rot.reshape(BATCH, DRAFT, KV * HD).astype(jnp.bfloat16)
    value_new = project(value_weight).astype(jnp.bfloat16)
    attended = lax.map(lambda packet: attend_row(*packet), (query_rot, key_rot, value_new, key_cache, value_cache, lengths))
    mixed = jnp.dot(attended.reshape(BATCH * DRAFT, HEADS * HD), out_weight, preferred_element_type=jnp.float32)
    return mixed.reshape(BATCH, DRAFT, D).astype(jnp.bfloat16)
```

```python
import math

import jax
import jax.numpy as jnp
from jax import lax
from jax.experimental import pallas as pl
from jax.experimental.pallas import tpu as pltpu
from jax.sharding import PartitionSpec as P

D = 8192
HD = 128
KV = 8
CTX = 4096
DRAFT = 16
QA = 512
QB = 768
MESH = pl.DeviceIdType.MESH
F32 = jnp.float32
BF = jnp.bfloat16


def wrap(value, size=4):
    return lax.rem(value + size, size)


class Place:
    def __init__(self):
        gx, gy = lax.axis_index("gx"), lax.axis_index("gy")
        self.gx, self.gy = gx, gy
        self.z, self.y = lax.div(gx, 4), lax.rem(gx, 4)
        self.x, self.c = lax.div(gy, 2), lax.rem(gy, 2)
        self.sibling = (gx, gy + 1 - 2 * self.c)

    def at_x(self, step):
        return (self.gx, wrap(self.x + step) * 2 + self.c)

    def at_y(self, step):
        return (self.z * 4 + wrap(self.y + step), self.gy)

    def at_z(self, step):
        return (wrap(self.z + step) * 4 + self.y, self.gy)

    def at_gy(self, step):
        return (self.gx, wrap(self.gy + step, 8))


class Net:
    def __init__(self, send_sem, recv_sem):
        self.send_sem, self.recv_sem = send_sem, recv_sem
        self.made = []

    def send(self, src, dst, device):
        index = len(self.made)
        copy = pltpu.make_async_remote_copy(
            src_ref=src,
            dst_ref=dst,
            send_sem=self.send_sem.at[index],
            recv_sem=self.recv_sem.at[index],
            device_id=device,
            device_id_type=MESH,
        )
        copy.start()
        self.made.append(copy)
        return copy

    def drain(self):
        for copy in self.made:
            copy.wait_send()


def greet(devices):
    barrier = pltpu.get_barrier_semaphore()
    for device in devices:
        pl.semaphore_signal(barrier, inc=1, device_id=device, device_id_type=MESH)
    pl.semaphore_wait(barrier, len(devices))


class RingSum:
    def __init__(self, net, get, plus, minus, bufs, lead, rows):
        self.net, self.get, self.plus, self.minus = net, get, plus, minus
        self.rows, self.half = rows, rows // 2
        self.so, self.sp, self.sm, self.rom, self.rop, self.rdm, self.rdp, self.kp, self.km = [
            buf.at[lead] for buf in bufs
        ]

    def start(self):
        h, r, net = self.half, self.rows, self.net
        lo, hi = pl.ds(0, h), pl.ds(h, h)
        self.so[...] = self.get(2).astype(BF)
        self.c_om = net.send(self.so.at[lo], self.rom, self.plus)
        self.c_op = net.send(self.so.at[hi], self.rop, self.minus)
        part = self.get(1)
        self.kp[...] = part[:h]
        self.sp[hi] = part[h:].astype(BF)
        self.c_dm1 = net.send(self.sp.at[hi], self.rdm.at[hi], self.plus)
        part = self.get(3)
        self.km[...] = part[h:]
        self.sm[lo] = part[:h].astype(BF)
        self.c_dp1 = net.send(self.sm.at[lo], self.rdp.at[lo], self.minus)

    def mid(self):
        h, net = self.half, self.net
        lo, hi = pl.ds(0, h), pl.ds(h, h)
        self.c_om.wait_recv()
        self.sp[lo] = (self.kp[...] + self.rom[...].astype(F32)).astype(BF)
        self.c_dm2 = net.send(self.sp.at[lo], self.rdm.at[lo], self.plus)
        self.c_op.wait_recv()
        self.sm[hi] = (self.km[...] + self.rop[...].astype(F32)).astype(BF)
        self.c_dp2 = net.send(self.sm.at[hi], self.rdp.at[hi], self.minus)

    def finish(self):
        own = self.get(0)
        for copy in (self.c_dm1, self.c_dp1, self.c_dm2, self.c_dp2):
            copy.wait_recv()
        return own + self.rdm[...].astype(F32) + self.rdp[...].astype(F32)


def ring_scratch(count, rows, cols):
    h = rows // 2
    return [
        pltpu.VMEM((count, rows, cols), BF),
        pltpu.VMEM((count, rows, cols), BF),
        pltpu.VMEM((count, rows, cols), BF),
        pltpu.VMEM((count, h, cols), BF),
        pltpu.VMEM((count, h, cols), BF),
        pltpu.VMEM((count, rows, cols), BF),
        pltpu.VMEM((count, rows, cols), BF),
        pltpu.VMEM((count, h, cols), F32),
        pltpu.VMEM((count, h, cols), F32),
    ]


K1_COPIES = 90


def project_kernel(
    act_h, gain_ref, wq_h, wk_h, wv_h, tab_h, out_ref,
    act, scaled, w, tab, sqall, sqr1, sqs, sqr2, sum_a, sum_b, sendq, recvq,
    *rest,
):
    bufs_a, bufs_b, bufs_a2, bufs_b2 = rest[0:9], rest[9:18], rest[18:27], rest[27:36]
    send_sem, recv_sem, local_sem = rest[36:]
    me = Place()
    x, c, y, z = me.x, me.c, me.y, me.z
    net = Net(send_sem, recv_sem)

    own_in = pltpu.make_async_copy(act_h, act.at[0, c], local_sem.at[0])
    own_in.start()
    w_in = [
        pltpu.make_async_copy(wq_h, w.at[:, pl.ds(0, 1024)], local_sem.at[1]),
        pltpu.make_async_copy(wk_h, w.at[:, pl.ds(1024, 128)], local_sem.at[2]),
        pltpu.make_async_copy(wv_h, w.at[:, pl.ds(1152, 128)], local_sem.at[3]),
    ]
    for copy in w_in:
        copy.start()
    tab_in = pltpu.make_async_copy(tab_h, tab.at[me.gy], local_sem.at[4])
    tab_in.start()

    greet(
        [me.at_gy(step) for step in range(1, 8)]
        + [me.at_y(step) for step in range(1, 4)]
        + [me.at_z(step) for step in range(1, 4)]
    )

    top, low = pl.ds(0, 128), pl.ds(128, 128)
    c_sib = net.send(act_h, act.at[0, c], me.sibling)
    c_1a = net.send(act_h.at[top], act.at[3, c, top], me.at_x(1))
    c_2a = net.send(act_h.at[low], act.at[1, c, low], me.at_x(-1))
    c_1b = net.send(act_h.at[low], act.at[3, c, low], me.at_x(1))
    c_2b = net.send(act_h.at[top], act.at[1, c, top], me.at_x(-1))
    c_tab = [net.send(tab_h, tab.at[me.gy], me.at_gy(step)) for step in range(1, 8)]

    gain = gain_ref[...].astype(F32)

    def prep(slot, core):
        for half in range(2):
            wide = act[slot, core, pl.ds(half * 128, 128), :].astype(F32)
            scaled[slot, core, pl.ds(half * 128, 128), :] = (wide * gain).astype(BF)
            square = wide * wide
            fold = (square[:, 0:128] + square[:, 128:256]) + (square[:, 256:384] + square[:, 384:512])
            row = jnp.sum(jnp.transpose(fold), axis=0, keepdims=True)
            sqall[2 * core + half, pl.ds(wrap(x + slot), 1), :] = row

    def rows_of(slot, yy):
        return scaled[slot, lax.div(yy, 2), pl.ds(pl.multiple_of(lax.rem(yy, 2) * 128, 128), 128), :]

    def get_b(slot):
        def get(role):
            return jnp.dot(rows_of(slot, wrap(y + role)), w[:, QA:], preferred_element_type=F32)
        return get

    def get_a(yrole):
        def get(role):
            slot = wrap(z + role - x + 4)
            return jnp.dot(rows_of(slot, wrap(y + yrole)), w[:, :QA], preferred_element_type=F32)
        return get

    ring_b = [RingSum(net, get_b(k), me.at_y(1), me.at_y(-1), bufs_b, k, 128) for k in range(4)]
    ring_a = [RingSum(net, get_a(k), me.at_z(1), me.at_z(-1), bufs_a, k, 128) for k in range(4)]
    ring_a2 = RingSum(net, lambda role: sum_a[role], me.at_y(1), me.at_y(-1), bufs_a2, 0, 128)
    ring_b2 = RingSum(
        net, lambda role: sum_b[wrap(z + role - x + 4)], me.at_z(1), me.at_z(-1), bufs_b2, 0, 128
    )

    own_in.wait()
    prep(0, c)
    for copy in w_in:
        copy.wait()
    c_sib.wait_recv()
    prep(0, 1 - c)
    ring_b[0].start()
    c_1a.wait_recv()
    c_r1 = net.send(act.at[3, c, top], act.at[2, c, top], me.at_x(1))
    c_2a.wait_recv()
    c_r2 = net.send(act.at[1, c, low], act.at[2, c, low], me.at_x(-1))
    ring_b[0].mid()
    c_1b.wait_recv()
    c_s3 = net.send(act.at[3, c], act.at[3, c], me.sibling)
    c_2b.wait_recv()
    c_s1 = net.send(act.at[1, c], act.at[1, c], me.sibling)
    prep(3, c)
    prep(1, c)
    c_s3.wait_recv()
    prep(3, 1 - c)
    ring_b[3].start()
    c_s1.wait_recv()
    prep(1, 1 - c)
    ring_b[1].start()
    sum_b[0] = ring_b[0].finish()
    c_r1.wait_recv()
    c_r2.wait_recv()
    c_s2 = net.send(act.at[2, c], act.at[2, c], me.sibling)
    prep(2, c)
    ring_b[3].mid()
    c_s2.wait_recv()
    prep(2, 1 - c)
    ring_a[2].start()
    ring_b[2].start()
    ring_b[1].mid()
    sq1 = [
        net.send(sqall.at[wrap(y + step)], sqr1.at[step - 1], me.at_y(step)) for step in range(1, 4)
    ]
    ring_a[1].start()
    sum_b[3] = ring_b[3].finish()
    ring_a[2].mid()
    ring_a[3].start()
    ring_b[2].mid()
    sum_b[1] = ring_b[1].finish()
    ring_a[0].start()
    ring_a[1].mid()
    sum_a[2] = ring_a[2].finish()
    for copy in sq1:
        copy.wait_recv()
    sqs[...] = (sqall[y] + sqr1[0]) + (sqr1[1] + sqr1[2])
    sq2 = [net.send(sqs, sqr2.at[step - 1], me.at_z(step)) for step in range(1, 4)]
    ring_a[3].mid()
    sum_b[2] = ring_b[2].finish()
    ring_b2.start()
    sum_a[1] = ring_a[1].finish()
    ring_a[0].mid()
    sum_a[3] = ring_a[3].finish()
    ring_a2.start()
    for copy in sq2:
        copy.wait_recv()
    totals = (sqs[...] + sqr2[0]) + (sqr2[1] + sqr2[2])
    sqs2 = sqr1.at[0]
    sqs2[...] = totals
    own_sq = sqs2[pl.ds(z, 1), :]
    inverse = jnp.transpose(jnp.broadcast_to(lax.rsqrt(own_sq / D + 1e-05), (128, 128)))
    tab_in.wait()
    for copy in c_tab:
        copy.wait_recv()
    both = tab[...].reshape(128, 128)
    turned = pltpu.roll(both, 64, 1)
    first = lax.broadcasted_iota(jnp.int32, (128, 128), 1) < 64
    cosine = jnp.where(first, both, turned)
    sine = jnp.where(first, -turned, both)
    sum_a[0] = ring_a[0].finish()
    ring_b2.mid()
    ring_a2.mid()

    def put(col, block):
        sendq[:, :, pl.ds(col, 128)] = block.astype(BF).reshape(8, 16, 128)

    def rotated(part):
        part = part * inverse
        return part * cosine + pltpu.roll(part, 64, 1) * sine

    fin = ring_b2.finish()
    for head in range(4):
        put(512 + head * 128, rotated(fin[:, head * 128 : (head + 1) * 128]))
    put(1024, rotated(fin[:, 512:640]))
    put(1152, fin[:, 640:768] * inverse)
    fin = ring_a2.finish()
    for head in range(4):
        put(head * 128, rotated(fin[:, head * 128 : (head + 1) * 128]))
    sends = [
        net.send(sendq.at[wrap(me.gy + step, 8)], recvq.at[me.gy], me.at_gy(step))
        for step in range(1, 8)
    ]
    recvq[me.gy] = sendq[me.gy]
    for copy in sends:
        copy.wait_recv()
    out_ref[...] = recvq[...]
    net.drain()
    assert len(net.made) == K1_COPIES


def project(act, gain, wq, wk, wv, tab):
    hbm = pl.BlockSpec(memory_space=pl.ANY)
    vmem = pl.BlockSpec(memory_space=pltpu.VMEM)
    return pl.pallas_call(
        project_kernel,
        out_shape=jax.ShapeDtypeStruct((8, DRAFT, 1280), BF),
        in_specs=[hbm, vmem, hbm, hbm, hbm, hbm],
        out_specs=vmem,
        scratch_shapes=[
            pltpu.VMEM((4, 2, 256, 512), BF),
            pltpu.VMEM((4, 2, 256, 512), BF),
            pltpu.VMEM((512, 1280), BF),
            pltpu.VMEM((8, 16, 128), F32),
            pltpu.VMEM((4, 8, 128), F32),
            pltpu.VMEM((3, 8, 128), F32),
            pltpu.VMEM((8, 128), F32),
            pltpu.VMEM((3, 8, 128), F32),
            pltpu.VMEM((4, 128, QA), F32),
            pltpu.VMEM((4, 128, QB), F32),
            pltpu.VMEM((8, 16, 1280), BF),
            pltpu.VMEM((8, 16, 1280), BF),
            *ring_scratch(4, 128, QA),
            *ring_scratch(4, 128, QB),
            *ring_scratch(1, 128, QA),
            *ring_scratch(1, 128, QB),
            pltpu.SemaphoreType.DMA((K1_COPIES,)),
            pltpu.SemaphoreType.DMA((K1_COPIES,)),
            pltpu.SemaphoreType.DMA((5,)),
        ],
        compiler_params=pltpu.CompilerParams(
            collective_id=0, has_side_effects=True, vmem_limit_bytes=56 * 1024 * 1024
        ),
        name="project",
    )(act, gain, wq, wk, wv, tab)


LOG2E = 1.4426950408889634


def attend_kernel(len_ref, qkv_ref, k_ref, v_ref, out_ref):
    packed = qkv_ref[0]
    query = jnp.concatenate([packed[:, h * 128 : (h + 1) * 128] for h in range(8)], axis=0)
    fresh_key, fresh_value = packed[:, 1024:1152], packed[:, 1152:1280]
    scale = HD ** (-0.5) * LOG2E
    contract = (((1,), (1,)), ((), ()))
    old = lax.dot_general(query, k_ref[0], contract, preferred_element_type=F32) * scale
    new = lax.dot_general(query, fresh_key, contract, preferred_element_type=F32) * scale
    old = jnp.where(lax.broadcasted_iota(jnp.int32, (1, CTX), 1) < len_ref[0], old, -1e30)
    token = lax.rem(lax.broadcasted_iota(jnp.int32, (128, 16), 0), 16)
    causal = lax.broadcasted_iota(jnp.int32, (128, 16), 1) <= token
    new = jnp.where(causal, new, -1e30)
    highest = jnp.maximum(
        jnp.max(old, axis=1, keepdims=True), jnp.max(new, axis=1, keepdims=True)
    )
    old = jnp.exp2(old - highest)
    new = jnp.exp2(new - highest)
    total = jnp.sum(old, axis=1, keepdims=True) + jnp.sum(new, axis=1, keepdims=True)
    blend = jnp.dot(old.astype(BF), v_ref[0], preferred_element_type=F32)
    blend = blend + jnp.dot(new.astype(BF), fresh_value, preferred_element_type=F32)
    result = (blend / total).astype(BF)
    out_ref[0] = jnp.concatenate([result[h * 16 : (h + 1) * 16] for h in range(8)], axis=1)


def attend(lengths, qkv, key_cache, value_cache):
    return pl.pallas_call(
        attend_kernel,
        out_shape=jax.ShapeDtypeStruct((8, DRAFT, 1024), BF),
        grid=(8,),
        in_specs=[
            pl.BlockSpec(memory_space=pltpu.SMEM),
            pl.BlockSpec((1, DRAFT, 1280), lambda g: (g, 0, 0)),
            pl.BlockSpec((1, CTX, 128), lambda g: (0, 0, g)),
            pl.BlockSpec((1, CTX, 128), lambda g: (0, 0, g)),
        ],
        out_specs=pl.BlockSpec((1, DRAFT, 1024), lambda g: (g, 0, 0)),
        compiler_params=pltpu.CompilerParams(vmem_limit_bytes=56 * 1024 * 1024),
        name="attend",
    )(lengths, qkv, key_cache, value_cache)


def places_table(position):
    frequency = jnp.exp(
        jnp.arange(64, dtype=F32) * (-2.0 * math.log(500000.0) / HD)
    )
    places = position + jnp.arange(DRAFT, dtype=jnp.int32)
    angles = places.astype(F32)[:, None] * frequency
    return jnp.concatenate([jnp.cos(angles), jnp.sin(angles)], axis=-1)


def shards(act, gain, wq, wk, wv, wo, key_cache, value_cache, lengths, positions):
    act = act.reshape(256, 512)
    qkv = project(act, gain.reshape(1, 512), wq, wk, wv, places_table(positions))
    attended = attend(lengths, qkv, key_cache, value_cache)
    regrouped = lax.all_to_all(attended, "gy", split_axis=0, concat_axis=0, tiled=True)
    gathered = lax.all_gather(regrouped, "gx", axis=0, tiled=True)
    terms = jnp.einsum("btf,fd->btd", gathered, wo, preferred_element_type=F32)
    return lax.psum_scatter(terms.astype(BF), "gy", scatter_dimension=0, tiled=True)


def solution(mesh):
    return jax.shard_map(
        shards,
        mesh=mesh,
        in_specs=(
            P("gy", None, "gx"),
            P("gx"),
            P("gx", "gy"),
            P("gx", "gy"),
            P("gx", "gy"),
            P("gy", "gx"),
            P(("gx", "gy"), None, None),
            P(("gx", "gy"), None, None),
            P(("gx", "gy")),
            P(("gx", "gy")),
        ),
        out_specs=P("gy", None, "gx"),
        check_vma=False,
    )
```

```python
import math

import jax
import jax.numpy as jnp
from jax import lax
from jax.experimental import pallas as pl
from jax.experimental.pallas import tpu as pltpu
from jax.sharding import PartitionSpec as P

D = 8192
HD = 128
KV = 8
CTX = 4096
DRAFT = 16
QA = 512
QB = 768
MESH = pl.DeviceIdType.MESH
F32 = jnp.float32
BF = jnp.bfloat16


def wrap(value, size=4):
    return lax.rem(value + size, size)


class Place:
    def __init__(self):
        gx, gy = lax.axis_index("gx"), lax.axis_index("gy")
        self.gx, self.gy = gx, gy
        self.z, self.y = lax.div(gx, 4), lax.rem(gx, 4)
        self.x, self.c = lax.div(gy, 2), lax.rem(gy, 2)
        self.sibling = (gx, gy + 1 - 2 * self.c)

    def at_x(self, step):
        return (self.gx, wrap(self.x + step) * 2 + self.c)

    def at_y(self, step):
        return (self.z * 4 + wrap(self.y + step), self.gy)

    def at_z(self, step):
        return (wrap(self.z + step) * 4 + self.y, self.gy)

    def at_gy(self, step):
        return (self.gx, wrap(self.gy + step, 8))


class Net:
    def __init__(self, send_sem, recv_sem):
        self.send_sem, self.recv_sem = send_sem, recv_sem
        self.made = []

    def send(self, src, dst, device):
        index = len(self.made)
        copy = pltpu.make_async_remote_copy(
            src_ref=src,
            dst_ref=dst,
            send_sem=self.send_sem.at[index],
            recv_sem=self.recv_sem.at[index],
            device_id=device,
            device_id_type=MESH,
        )
        copy.start()
        self.made.append(copy)
        return copy

    def drain(self):
        for copy in self.made:
            copy.wait_send()


def greet(devices):
    barrier = pltpu.get_barrier_semaphore()
    for device in devices:
        pl.semaphore_signal(barrier, inc=1, device_id=device, device_id_type=MESH)
    pl.semaphore_wait(barrier, len(devices))


class RingSum:
    def __init__(self, net, get, plus, minus, bufs, lead, rows):
        self.net, self.get, self.plus, self.minus = net, get, plus, minus
        self.rows, self.half = rows, rows // 2
        self.so, self.sp, self.sm, self.rom, self.rop, self.rdm, self.rdp, self.kp, self.km = [
            buf.at[lead] for buf in bufs
        ]

    def start(self):
        h, r, net = self.half, self.rows, self.net
        lo, hi = pl.ds(0, h), pl.ds(h, h)
        self.so[...] = self.get(2).astype(BF)
        self.c_om = net.send(self.so.at[lo], self.rom, self.plus)
        self.c_op = net.send(self.so.at[hi], self.rop, self.minus)
        part = self.get(1)
        self.kp[...] = part[:h]
        self.sp[hi] = part[h:].astype(BF)
        self.c_dm1 = net.send(self.sp.at[hi], self.rdm.at[hi], self.plus)
        part = self.get(3)
        self.km[...] = part[h:]
        self.sm[lo] = part[:h].astype(BF)
        self.c_dp1 = net.send(self.sm.at[lo], self.rdp.at[lo], self.minus)

    def mid(self):
        h, net = self.half, self.net
        lo, hi = pl.ds(0, h), pl.ds(h, h)
        self.c_om.wait_recv()
        self.sp[lo] = (self.kp[...] + self.rom[...].astype(F32)).astype(BF)
        self.c_dm2 = net.send(self.sp.at[lo], self.rdm.at[lo], self.plus)
        self.c_op.wait_recv()
        self.sm[hi] = (self.km[...] + self.rop[...].astype(F32)).astype(BF)
        self.c_dp2 = net.send(self.sm.at[hi], self.rdp.at[hi], self.minus)

    def finish(self):
        own = self.get(0)
        for copy in (self.c_dm1, self.c_dp1, self.c_dm2, self.c_dp2):
            copy.wait_recv()
        return own + self.rdm[...].astype(F32) + self.rdp[...].astype(F32)


def ring_scratch(count, rows, cols):
    h = rows // 2
    return [
        pltpu.VMEM((count, rows, cols), BF),
        pltpu.VMEM((count, rows, cols), BF),
        pltpu.VMEM((count, rows, cols), BF),
        pltpu.VMEM((count, h, cols), BF),
        pltpu.VMEM((count, h, cols), BF),
        pltpu.VMEM((count, rows, cols), BF),
        pltpu.VMEM((count, rows, cols), BF),
        pltpu.VMEM((count, h, cols), F32),
        pltpu.VMEM((count, h, cols), F32),
    ]


K1_COPIES = 90


def project_kernel(
    act_h, gain_ref, wq_h, wk_h, wv_h, tab_h, out_ref,
    act, scaled, w, tab, sqall, sqr1, sqs, sqr2, sum_a, sum_b, sendq, recvq,
    *rest,
):
    bufs_a, bufs_b, bufs_a2, bufs_b2 = rest[0:9], rest[9:18], rest[18:27], rest[27:36]
    send_sem, recv_sem, local_sem = rest[36:]
    me = Place()
    x, c, y, z = me.x, me.c, me.y, me.z
    net = Net(send_sem, recv_sem)

    own_in = pltpu.make_async_copy(act_h, act.at[0, c], local_sem.at[0])
    own_in.start()
    w_in = [
        pltpu.make_async_copy(wq_h, w.at[:, pl.ds(0, 1024)], local_sem.at[1]),
        pltpu.make_async_copy(wk_h, w.at[:, pl.ds(1024, 128)], local_sem.at[2]),
        pltpu.make_async_copy(wv_h, w.at[:, pl.ds(1152, 128)], local_sem.at[3]),
    ]
    for copy in w_in:
        copy.start()
    tab_in = pltpu.make_async_copy(tab_h, tab.at[me.gy], local_sem.at[4])
    tab_in.start()

    greet(
        [me.at_gy(step) for step in range(1, 8)]
        + [me.at_y(step) for step in range(1, 4)]
        + [me.at_z(step) for step in range(1, 4)]
    )

    top, low = pl.ds(0, 128), pl.ds(128, 128)
    c_sib = net.send(act_h, act.at[0, c], me.sibling)
    c_1a = net.send(act_h.at[top], act.at[3, c, top], me.at_x(1))
    c_2a = net.send(act_h.at[low], act.at[1, c, low], me.at_x(-1))
    c_1b = net.send(act_h.at[low], act.at[3, c, low], me.at_x(1))
    c_2b = net.send(act_h.at[top], act.at[1, c, top], me.at_x(-1))
    c_tab = [net.send(tab_h, tab.at[me.gy], me.at_gy(step)) for step in range(1, 8)]

    gain = gain_ref[...].astype(F32)

    def prep(slot, core):
        for half in range(2):
            wide = act[slot, core, pl.ds(half * 128, 128), :].astype(F32)
            scaled[slot, core, pl.ds(half * 128, 128), :] = (wide * gain).astype(BF)
            square = wide * wide
            fold = (square[:, 0:128] + square[:, 128:256]) + (square[:, 256:384] + square[:, 384:512])
            row = jnp.sum(jnp.transpose(fold), axis=0, keepdims=True)
            sqall[2 * core + half, pl.ds(wrap(x + slot), 1), :] = row

    def rows_of(slot, yy):
        return scaled[slot, lax.div(yy, 2), pl.ds(pl.multiple_of(lax.rem(yy, 2) * 128, 128), 128), :]

    def get_b(slot):
        def get(role):
            return jnp.dot(rows_of(slot, wrap(y + role)), w[:, QA:], preferred_element_type=F32)
        return get

    def get_a(yrole):
        def get(role):
            slot = wrap(z + role - x + 4)
            return jnp.dot(rows_of(slot, wrap(y + yrole)), w[:, :QA], preferred_element_type=F32)
        return get

    ring_b = [RingSum(net, get_b(k), me.at_y(1), me.at_y(-1), bufs_b, k, 128) for k in range(4)]
    ring_a = [RingSum(net, get_a(k), me.at_z(1), me.at_z(-1), bufs_a, k, 128) for k in range(4)]
    ring_a2 = RingSum(net, lambda role: sum_a[role], me.at_y(1), me.at_y(-1), bufs_a2, 0, 128)
    ring_b2 = RingSum(
        net, lambda role: sum_b[wrap(z + role - x + 4)], me.at_z(1), me.at_z(-1), bufs_b2, 0, 128
    )

    own_in.wait()
    prep(0, c)
    for copy in w_in:
        copy.wait()
    c_sib.wait_recv()
    prep(0, 1 - c)
    ring_b[0].start()
    c_1a.wait_recv()
    c_r1 = net.send(act.at[3, c, top], act.at[2, c, top], me.at_x(1))
    c_2a.wait_recv()
    c_r2 = net.send(act.at[1, c, low], act.at[2, c, low], me.at_x(-1))
    ring_b[0].mid()
    c_1b.wait_recv()
    c_s3 = net.send(act.at[3, c], act.at[3, c], me.sibling)
    c_2b.wait_recv()
    c_s1 = net.send(act.at[1, c], act.at[1, c], me.sibling)
    prep(3, c)
    prep(1, c)
    c_s3.wait_recv()
    prep(3, 1 - c)
    ring_b[3].start()
    c_s1.wait_recv()
    prep(1, 1 - c)
    ring_b[1].start()
    sum_b[0] = ring_b[0].finish()
    c_r1.wait_recv()
    c_r2.wait_recv()
    c_s2 = net.send(act.at[2, c], act.at[2, c], me.sibling)
    prep(2, c)
    ring_b[3].mid()
    c_s2.wait_recv()
    prep(2, 1 - c)
    ring_a[2].start()
    ring_b[2].start()
    ring_b[1].mid()
    sq1 = [
        net.send(sqall.at[wrap(y + step)], sqr1.at[step - 1], me.at_y(step)) for step in range(1, 4)
    ]
    ring_a[1].start()
    sum_b[3] = ring_b[3].finish()
    ring_a[2].mid()
    ring_a[3].start()
    ring_b[2].mid()
    sum_b[1] = ring_b[1].finish()
    ring_a[0].start()
    ring_a[1].mid()
    sum_a[2] = ring_a[2].finish()
    for copy in sq1:
        copy.wait_recv()
    sqs[...] = (sqall[y] + sqr1[0]) + (sqr1[1] + sqr1[2])
    sq2 = [net.send(sqs, sqr2.at[step - 1], me.at_z(step)) for step in range(1, 4)]
    ring_a[3].mid()
    sum_b[2] = ring_b[2].finish()
    ring_b2.start()
    sum_a[1] = ring_a[1].finish()
    ring_a[0].mid()
    sum_a[3] = ring_a[3].finish()
    ring_a2.start()
    for copy in sq2:
        copy.wait_recv()
    totals = (sqs[...] + sqr2[0]) + (sqr2[1] + sqr2[2])
    sqs2 = sqr1.at[0]
    sqs2[...] = totals
    own_sq = sqs2[pl.ds(z, 1), :]
    inverse = jnp.transpose(jnp.broadcast_to(lax.rsqrt(own_sq / D + 1e-05), (128, 128)))
    tab_in.wait()
    for copy in c_tab:
        copy.wait_recv()
    both = tab[...].reshape(128, 128)
    turned = pltpu.roll(both, 64, 1)
    first = lax.broadcasted_iota(jnp.int32, (128, 128), 1) < 64
    cosine = jnp.where(first, both, turned)
    sine = jnp.where(first, -turned, both)
    sum_a[0] = ring_a[0].finish()
    ring_b2.mid()
    ring_a2.mid()

    def put(col, block):
        sendq[:, :, pl.ds(col, 128)] = block.astype(BF).reshape(8, 16, 128)

    def rotated(part):
        part = part * inverse
        return part * cosine + pltpu.roll(part, 64, 1) * sine

    fin = ring_b2.finish()
    for head in range(4):
        put(512 + head * 128, rotated(fin[:, head * 128 : (head + 1) * 128]))
    put(1024, rotated(fin[:, 512:640]))
    put(1152, fin[:, 640:768] * inverse)
    fin = ring_a2.finish()
    for head in range(4):
        put(head * 128, rotated(fin[:, head * 128 : (head + 1) * 128]))
    sends = [
        net.send(sendq.at[wrap(me.gy + step, 8)], recvq.at[me.gy], me.at_gy(step))
        for step in range(1, 8)
    ]
    recvq[me.gy] = sendq[me.gy]
    for copy in sends:
        copy.wait_recv()
    out_ref[...] = recvq[...]
    net.drain()
    assert len(net.made) == K1_COPIES


def project(act, gain, wq, wk, wv, tab):
    hbm = pl.BlockSpec(memory_space=pl.ANY)
    vmem = pl.BlockSpec(memory_space=pltpu.VMEM)
    return pl.pallas_call(
        project_kernel,
        out_shape=jax.ShapeDtypeStruct((8, DRAFT, 1280), BF),
        in_specs=[hbm, vmem, hbm, hbm, hbm, hbm],
        out_specs=vmem,
        scratch_shapes=[
            pltpu.VMEM((4, 2, 256, 512), BF),
            pltpu.VMEM((4, 2, 256, 512), BF),
            pltpu.VMEM((512, 1280), BF),
            pltpu.VMEM((8, 16, 128), F32),
            pltpu.VMEM((4, 8, 128), F32),
            pltpu.VMEM((3, 8, 128), F32),
            pltpu.VMEM((8, 128), F32),
            pltpu.VMEM((3, 8, 128), F32),
            pltpu.VMEM((4, 128, QA), F32),
            pltpu.VMEM((4, 128, QB), F32),
            pltpu.VMEM((8, 16, 1280), BF),
            pltpu.VMEM((8, 16, 1280), BF),
            *ring_scratch(4, 128, QA),
            *ring_scratch(4, 128, QB),
            *ring_scratch(1, 128, QA),
            *ring_scratch(1, 128, QB),
            pltpu.SemaphoreType.DMA((K1_COPIES,)),
            pltpu.SemaphoreType.DMA((K1_COPIES,)),
            pltpu.SemaphoreType.DMA((5,)),
        ],
        compiler_params=pltpu.CompilerParams(
            collective_id=0, has_side_effects=True, vmem_limit_bytes=56 * 1024 * 1024
        ),
        name="project",
    )(act, gain, wq, wk, wv, tab)


LOG2E = 1.4426950408889634


def attend_kernel(len_ref, qkv_ref, k_ref, v_ref, out_ref):
    packed = qkv_ref[0]
    query = jnp.concatenate([packed[:, h * 128 : (h + 1) * 128] for h in range(8)], axis=0)
    fresh_key, fresh_value = packed[:, 1024:1152], packed[:, 1152:1280]
    scale = HD ** (-0.5) * LOG2E
    contract = (((1,), (1,)), ((), ()))
    old = lax.dot_general(query, k_ref[0], contract, preferred_element_type=F32) * scale
    new = lax.dot_general(query, fresh_key, contract, preferred_element_type=F32) * scale
    old = jnp.where(lax.broadcasted_iota(jnp.int32, (1, CTX), 1) < len_ref[0], old, -1e30)
    token = lax.rem(lax.broadcasted_iota(jnp.int32, (128, 16), 0), 16)
    causal = lax.broadcasted_iota(jnp.int32, (128, 16), 1) <= token
    new = jnp.where(causal, new, -1e30)
    highest = jnp.maximum(
        jnp.max(old, axis=1, keepdims=True), jnp.max(new, axis=1, keepdims=True)
    )
    old = jnp.exp2(old - highest)
    new = jnp.exp2(new - highest)
    total = jnp.sum(old, axis=1, keepdims=True) + jnp.sum(new, axis=1, keepdims=True)
    blend = jnp.dot(old.astype(BF), v_ref[0], preferred_element_type=F32)
    blend = blend + jnp.dot(new.astype(BF), fresh_value, preferred_element_type=F32)
    result = (blend / total).astype(BF)
    out_ref[0] = jnp.concatenate([result[h * 16 : (h + 1) * 16] for h in range(8)], axis=1)


def attend(lengths, qkv, key_cache, value_cache):
    return pl.pallas_call(
        attend_kernel,
        out_shape=jax.ShapeDtypeStruct((8, DRAFT, 1024), BF),
        grid=(8,),
        in_specs=[
            pl.BlockSpec(memory_space=pltpu.SMEM),
            pl.BlockSpec((1, DRAFT, 1280), lambda g: (g, 0, 0)),
            pl.BlockSpec((1, CTX, 128), lambda g: (0, 0, g)),
            pl.BlockSpec((1, CTX, 128), lambda g: (0, 0, g)),
        ],
        out_specs=pl.BlockSpec((1, DRAFT, 1024), lambda g: (g, 0, 0)),
        compiler_params=pltpu.CompilerParams(vmem_limit_bytes=56 * 1024 * 1024),
        name="attend",
    )(lengths, qkv, key_cache, value_cache)


class RingCast:
    def __init__(self, net, slots, plus, minus):
        self.net, self.slots, self.plus, self.minus = net, slots, plus, minus
        self.lo, self.hi = pl.ds(0, 32), pl.ds(32, 32)

    def start(self):
        net, lo, hi = self.net, self.lo, self.hi
        own, next_, _, last = self.slots
        self.c_pl = net.send(own.at[lo], last.at[lo], self.plus)
        self.c_mh = net.send(own.at[hi], next_.at[hi], self.minus)
        self.c_ph = net.send(own.at[hi], last.at[hi], self.plus)
        self.c_ml = net.send(own.at[lo], next_.at[lo], self.minus)

    def relay(self):
        net, lo, hi = self.net, self.lo, self.hi
        _, next_, far, last = self.slots
        self.c_pl.wait_recv()
        self.c_rp = net.send(last.at[lo], far.at[lo], self.plus)
        self.c_mh.wait_recv()
        self.c_rm = net.send(next_.at[hi], far.at[hi], self.minus)

    def near(self):
        self.c_ph.wait_recv()
        self.c_ml.wait_recv()

    def far(self):
        self.c_rp.wait_recv()
        self.c_rm.wait_recv()


K3_COPIES = 77


def out_kernel(att_h, wo_h, out_ref, g, wo, part, sib_send, sib_recv, *rest):
    bufs = rest[0:9]
    send_sem, recv_sem, local_sem = rest[9:]
    me = Place()
    x, c, y, z = me.x, me.c, me.y, me.z
    net = Net(send_sem, recv_sem)
    w_in = pltpu.make_async_copy(wo_h, wo, local_sem.at[0])
    w_in.start()
    spot = pl.ds(pl.multiple_of(lax.rem(me.gy, 4) * 16, 16), 16)
    own_in = pltpu.make_async_copy(
        att_h.at[me.gy], g.at[lax.div(me.gy, 4), 0, 0, spot], local_sem.at[1]
    )
    own_in.start()
    greet(
        [me.at_gy(step) for step in range(1, 8)]
        + [me.at_y(1), me.at_y(-1), me.at_z(1), me.at_z(-1)]
    )
    swap = [
        net.send(
            att_h.at[wrap(me.gy + step, 8)], g.at[lax.div(me.gy, 4), 0, 0, spot], me.at_gy(step)
        )
        for step in range(1, 8)
    ]
    ym, yp, zm, zp = me.at_y(-1), me.at_y(1), me.at_z(-1), me.at_z(1)
    a1 = RingCast(net, [g.at[0, k, 0] for k in range(4)], zp, zm)
    b1 = RingCast(net, [g.at[1, 0, k] for k in range(4)], yp, ym)
    a2 = [RingCast(net, [g.at[0, j, k] for k in range(4)], yp, ym) for j in range(4)]
    b2 = [RingCast(net, [g.at[1, k, j] for k in range(4)], zp, zm) for j in range(4)]
    own_in.wait()
    for copy in swap:
        copy.wait_recv()
    a1.start()
    b1.start()
    a2[0].start()
    b2[0].start()
    a1.relay()
    b1.relay()
    a1.near()
    a2[1].start()
    a2[3].start()
    b1.near()
    b2[1].start()
    b2[3].start()
    a2[0].relay()
    b2[0].relay()
    a1.far()
    a2[2].start()
    b1.far()
    b2[2].start()
    a2[1].relay()
    b2[1].relay()
    a2[3].relay()
    b2[3].relay()
    w_in.wait()
    pair = [None] * 4

    def multiply(dz):
        for mine in (False, True):
            core = c if mine else 1 - c
            for half in range(2):
                rows = jnp.concatenate(
                    [g[half, dz, wrap(core * 2 + i - y)] for i in range(2)], axis=0
                )
                term = jnp.dot(rows, wo[...], preferred_element_type=F32)
                if mine:
                    part[dz, pl.ds(half * 128, 128), :] = term
                else:
                    sib_send[dz, pl.ds(half * 128, 128), :] = term.astype(BF)
            if not mine:
                pair[dz] = net.send(sib_send.at[dz], sib_recv.at[dz], me.sibling)

    a2[0].near()
    a2[0].far()
    multiply(0)
    a2[2].relay()
    b2[2].relay()
    for ring in a2[1], a2[3]:
        ring.near()
        ring.far()
    for ring in b2:
        ring.near()
    multiply(1)
    multiply(3)
    a2[2].near()
    a2[2].far()
    for ring in b2:
        ring.far()
    multiply(2)
    for copy in pair:
        copy.wait_recv()

    def get(role):
        dz = wrap(x + role - z + 4)
        return part[dz] + sib_recv[dz].astype(F32)

    ring = RingSum(net, get, me.at_x(1), me.at_x(-1), bufs, 0, 256)
    ring.start()
    ring.mid()
    done = ring.finish().astype(BF)
    for half in range(2):
        for i in range(2):
            out_ref[pl.ds(i * 128 + half * 64, 64), :] = done[
                half * 128 + i * 64 : half * 128 + i * 64 + 64
            ]
    net.drain()
    assert len(net.made) == K3_COPIES


def project_out(att, wo):
    hbm = pl.BlockSpec(memory_space=pl.ANY)
    vmem = pl.BlockSpec(memory_space=pltpu.VMEM)
    return pl.pallas_call(
        out_kernel,
        out_shape=jax.ShapeDtypeStruct((256, 512), BF),
        in_specs=[hbm, hbm],
        out_specs=vmem,
        scratch_shapes=[
            pltpu.VMEM((2, 4, 4, 64, 1024), BF),
            pltpu.VMEM((1024, 512), BF),
            pltpu.VMEM((4, 256, 512), F32),
            pltpu.VMEM((4, 256, 512), BF),
            pltpu.VMEM((4, 256, 512), BF),
            *ring_scratch(1, 256, 512),
            pltpu.SemaphoreType.DMA((K3_COPIES,)),
            pltpu.SemaphoreType.DMA((K3_COPIES,)),
            pltpu.SemaphoreType.DMA((2,)),
        ],
        compiler_params=pltpu.CompilerParams(
            collective_id=1, has_side_effects=True, vmem_limit_bytes=56 * 1024 * 1024
        ),
        name="project_out",
    )(att, wo)


def places_table(position):
    frequency = jnp.exp(
        jnp.arange(64, dtype=F32) * (-2.0 * math.log(500000.0) / HD)
    )
    places = position + jnp.arange(DRAFT, dtype=jnp.int32)
    angles = places.astype(F32)[:, None] * frequency
    return jnp.concatenate([jnp.cos(angles), jnp.sin(angles)], axis=-1)


def shards(act, gain, wq, wk, wv, wo, key_cache, value_cache, lengths, positions):
    act = act.reshape(256, 512)
    qkv = project(act, gain.reshape(1, 512), wq, wk, wv, places_table(positions))
    attended = attend(lengths, qkv, key_cache, value_cache)
    return project_out(attended, wo).reshape(16, DRAFT, 512)


def solution(mesh):
    return jax.shard_map(
        shards,
        mesh=mesh,
        in_specs=(
            P("gy", None, "gx"),
            P("gx"),
            P("gx", "gy"),
            P("gx", "gy"),
            P("gx", "gy"),
            P("gy", "gx"),
            P(("gx", "gy"), None, None),
            P(("gx", "gy"), None, None),
            P(("gx", "gy")),
            P(("gx", "gy")),
        ),
        out_specs=P("gy", None, "gx"),
        check_vma=False,
    )
```

```python
import math

import jax
import jax.numpy as jnp
from jax import lax
from jax.experimental import pallas as pl
from jax.experimental.pallas import tpu as pltpu
from jax.sharding import PartitionSpec as P

D = 8192
HD = 128
KV = 8
CTX = 4096
DRAFT = 16
MESH = pl.DeviceIdType.MESH
F32 = jnp.float32
BF = jnp.bfloat16


def wrap(value, size=4):
    return lax.rem(value + size, size)


class Place:
    def __init__(self):
        gx, gy = lax.axis_index("gx"), lax.axis_index("gy")
        self.gx, self.gy = gx, gy
        self.z, self.y = lax.div(gx, 4), lax.rem(gx, 4)
        self.x, self.c = lax.div(gy, 2), lax.rem(gy, 2)
        self.sibling = (gx, gy + 1 - 2 * self.c)

    def at_x(self, step):
        return (self.gx, wrap(self.x + step) * 2 + self.c)

    def at_y(self, step):
        return (self.z * 4 + wrap(self.y + step), self.gy)

    def at_z(self, step):
        return (wrap(self.z + step) * 4 + self.y, self.gy)

    def at_gy(self, step):
        return (self.gx, wrap(self.gy + step, 8))


class Net:
    def __init__(self, send_sem, recv_sem):
        self.send_sem, self.recv_sem = send_sem, recv_sem
        self.count = 0
        self.sent = []

    def make(self, src, dst, device, drained=True):
        copy = pltpu.make_async_remote_copy(
            src_ref=src,
            dst_ref=dst,
            send_sem=self.send_sem.at[self.count],
            recv_sem=self.recv_sem.at[self.count],
            device_id=device,
            device_id_type=MESH,
        )
        self.count += 1
        if drained:
            self.sent.append(copy)
        return copy

    def send(self, src, dst, device):
        copy = self.make(src, dst, device)
        copy.start()
        return copy

    def drain(self):
        for copy in self.sent:
            copy.wait_send()


def greet(devices):
    barrier = pltpu.get_barrier_semaphore()
    for device in devices:
        pl.semaphore_signal(barrier, inc=1, device_id=device, device_id_type=MESH)
    pl.semaphore_wait(barrier, len(devices))


class RingSum:
    def __init__(self, net, get, plus, minus, bufs, lead, rows, drained=True):
        self.get = get
        self.rows, self.half = rows, rows // 2
        self.so, self.sp, self.sm, self.rom, self.rop, self.rdm, self.rdp, self.kp, self.km = [
            buf.at[lead] for buf in bufs
        ]
        lo, hi = pl.ds(0, self.half), pl.ds(self.half, self.half)
        self.lo, self.hi = lo, hi
        self.om = net.make(self.so.at[lo], self.rom, plus, drained)
        self.op = net.make(self.so.at[hi], self.rop, minus, drained)
        self.m1 = net.make(self.sp.at[hi], self.rdm.at[hi], plus, drained)
        self.p1 = net.make(self.sm.at[lo], self.rdp.at[lo], minus, drained)
        self.m2 = net.make(self.sp.at[lo], self.rdm.at[lo], plus, drained)
        self.p2 = net.make(self.sm.at[hi], self.rdp.at[hi], minus, drained)
        self.copies = [self.om, self.op, self.m1, self.p1, self.m2, self.p2]

    def start(self):
        h = self.half
        self.so[...] = self.get(2).astype(BF)
        self.om.start()
        self.op.start()
        part = self.get(1)
        self.kp[...] = part[:h]
        self.sp[self.hi] = part[h:].astype(BF)
        self.m1.start()
        part = self.get(3)
        self.km[...] = part[h:]
        self.sm[self.lo] = part[:h].astype(BF)
        self.p1.start()

    def mid(self):
        self.om.wait_recv()
        self.sp[self.lo] = (self.kp[...] + self.rom[...].astype(F32)).astype(BF)
        self.m2.start()
        self.op.wait_recv()
        self.sm[self.hi] = (self.km[...] + self.rop[...].astype(F32)).astype(BF)
        self.p2.start()

    def finish(self):
        own = self.get(0)
        for copy in (self.m1, self.p1, self.m2, self.p2):
            copy.wait_recv()
        return own + self.rdm[...].astype(F32) + self.rdp[...].astype(F32)


def ring_scratch(count, rows, cols):
    h = rows // 2
    return [
        pltpu.VMEM((count, rows, cols), BF),
        pltpu.VMEM((count, rows, cols), BF),
        pltpu.VMEM((count, rows, cols), BF),
        pltpu.VMEM((count, h, cols), BF),
        pltpu.VMEM((count, h, cols), BF),
        pltpu.VMEM((count, rows, cols), BF),
        pltpu.VMEM((count, rows, cols), BF),
        pltpu.VMEM((count, h, cols), F32),
        pltpu.VMEM((count, h, cols), F32),
    ]


class BlockSum:
    def __init__(self, net, role, slot, plus, minus, bufs, parts, rows):
        self.role, self.slot, self.parts = role, slot, parts
        self.out, self.rom, self.rop, self.rdm, self.rdp, self.keep = bufs
        h = rows // 2
        lo, hi = pl.ds(0, h), pl.ds(h, h)
        self.lo, self.hi = lo, hi
        far, near, last = slot(2), slot(1), slot(3)
        span = range(parts)
        self.om = [net.make(self.out.at[far, j, lo], self.rom.at[j], plus) for j in span]
        self.op = [net.make(self.out.at[far, j, hi], self.rop.at[j], minus) for j in span]
        self.m1 = [net.make(self.out.at[near, j, hi], self.rdm.at[j, hi], plus) for j in span]
        self.p1 = [net.make(self.out.at[last, j, lo], self.rdp.at[j, lo], minus) for j in span]
        self.m2 = [net.make(self.out.at[near, j, lo], self.rdm.at[j, lo], plus) for j in span]
        self.p2 = [net.make(self.out.at[last, j, hi], self.rdp.at[j, hi], minus) for j in span]

    def block(self, k, get):
        role = self.role(k)
        for j in (2, 1, 3, 0)[-self.parts :] if self.parts == 4 else range(self.parts):
            value = get(j)
            self.out[k, j] = value.astype(BF)
            if self.keep is not None:
                self.keep[k, j] = value

            @pl.when(role == 2)
            def _():
                self.om[j].start()
                self.op[j].start()

            @pl.when(role == 1)
            def _():
                self.m1[j].start()

            @pl.when(role == 3)
            def _():
                self.p1[j].start()

    def value(self, k, j, rows):
        if self.keep is not None:
            return self.keep[k, j, rows]
        return self.out[k, j, rows].astype(F32)

    def mid(self, k):
        role = self.role(k)
        order = (2, 1, 3, 0) if self.parts == 4 else range(self.parts)

        @pl.when(role == 1)
        def _():
            for j in order:
                self.om[j].wait_recv()
                total = self.value(k, j, self.lo) + self.rom[j].astype(F32)
                self.out[k, j, self.lo] = total.astype(BF)
                self.m2[j].start()

        @pl.when(role == 3)
        def _():
            for j in order:
                self.op[j].wait_recv()
                total = self.value(k, j, self.hi) + self.rop[j].astype(F32)
                self.out[k, j, self.hi] = total.astype(BF)
                self.p2[j].start()

    def finish(self, j):
        own = self.value(self.slot(0), j, slice(None))
        for copy in (self.m1[j], self.p1[j], self.m2[j], self.p2[j]):
            copy.wait_recv()
        return own + self.rdm[j].astype(F32) + self.rdp[j].astype(F32)


def block_scratch(parts, rows, cols):
    return [
        pltpu.VMEM((4, parts, rows, cols), BF),
        pltpu.VMEM((parts, rows // 2, cols), BF),
        pltpu.VMEM((parts, rows // 2, cols), BF),
        pltpu.VMEM((parts, rows, cols), BF),
        pltpu.VMEM((parts, rows, cols), BF),
    ]


class RingCast:
    def __init__(self, net, slots, plus, minus):
        lo, hi = pl.ds(0, 32), pl.ds(32, 32)
        own, next_, far, last = slots
        self.pl = net.make(own.at[lo], last.at[lo], plus)
        self.mh = net.make(own.at[hi], next_.at[hi], minus)
        self.ph = net.make(own.at[hi], last.at[hi], plus)
        self.ml = net.make(own.at[lo], next_.at[lo], minus)
        self.rp = net.make(last.at[lo], far.at[lo], plus)
        self.rm = net.make(next_.at[hi], far.at[hi], minus)

    def start(self):
        for copy in (self.pl, self.mh, self.ph, self.ml):
            copy.start()

    def relay(self):
        self.pl.wait_recv()
        self.rp.start()
        self.mh.wait_recv()
        self.rm.start()

    def near(self):
        self.ph.wait_recv()
        self.ml.wait_recv()

    def far(self):
        self.rp.wait_recv()
        self.rm.wait_recv()


COLS = 640
COPIES = 192
CHUNK = 512


def layer_kernel(
    act_h, gain_ref, wq_h, wk_h, wv_h, wo_h, tab_h, len_ref, k_h, v_h, out_ref,
    act, scaled, w, tab, sqall, sqr1, sqs, sqr2, sendq, recvq, kv, vv, bias, score, att,
    g, wo, sib_send, sib_recv, keep_b, *rest,
):
    bufs_a, rest = rest[:5], rest[5:]
    bufs_b2, rest = rest[:5], rest[5:]
    bufs_b, rest = rest[:9], rest[9:]
    bufs_a2, rest = rest[:9], rest[9:]
    bufs_x, rest = rest[:9], rest[9:]
    send_sem, recv_sem, local_sem = rest
    me = Place()
    x, c, y, z, gy = me.x, me.c, me.y, me.z, me.gy
    net = Net(send_sem, recv_sem)
    ym, yp, zm, zp = me.at_y(-1), me.at_y(1), me.at_z(-1), me.at_z(1)

    local = []

    def fetch(src, dst):
        copy = pltpu.make_async_copy(src, dst, local_sem.at[len(local)])
        copy.start()
        local.append(copy)
        return copy

    own_in = fetch(act_h, act.at[0, c])
    w_in = [
        fetch(wq_h.at[:, pl.ds(0, 512)], w.at[:, pl.ds(0, 512)]),
        fetch(wk_h, w.at[:, pl.ds(512, 128)]),
        fetch(wq_h.at[:, pl.ds(512, 512)], w.at[:, pl.ds(640, 512)]),
        fetch(wv_h, w.at[:, pl.ds(1152, 128)]),
    ]
    tab_in = fetch(tab_h, tab.at[gy])

    greet(
        [me.at_gy(step) for step in range(1, 8)]
        + [me.at_y(step) for step in range(1, 4)]
        + [me.at_z(step) for step in range(1, 4)]
    )

    top, low = pl.ds(0, 128), pl.ds(128, 128)
    c_sib = net.send(act_h, act.at[0, c], me.sibling)
    c_1a = net.send(act_h.at[top], act.at[3, c, top], me.at_x(1))
    c_2a = net.send(act_h.at[low], act.at[1, c, low], me.at_x(-1))
    c_1b = net.send(act_h.at[low], act.at[3, c, low], me.at_x(1))
    c_2b = net.send(act_h.at[top], act.at[1, c, top], me.at_x(-1))
    c_tab = [net.send(tab_h, tab.at[gy], me.at_gy(step)) for step in range(1, 8)]

    gain = gain_ref[...].astype(F32)

    def prep(slot, core):
        for half in range(2):
            wide = act[slot, core, pl.ds(half * 128, 128), :].astype(F32)
            scaled[slot, core, pl.ds(half * 128, 128), :] = (wide * gain).astype(BF)
            square = wide * wide
            fold = (square[:, 0:128] + square[:, 128:256]) + (square[:, 256:384] + square[:, 384:512])
            row = jnp.sum(jnp.transpose(fold), axis=0, keepdims=True)
            sqall[2 * core + half, pl.ds(wrap(x + slot), 1), :] = row

    def rows_of(slot, yy):
        return scaled[slot, lax.div(yy, 2), pl.ds(pl.multiple_of(lax.rem(yy, 2) * 128, 128), 128), :]

    def get_b(slot):
        def get(role):
            return jnp.dot(rows_of(slot, wrap(y + role)), w[:, COLS:], preferred_element_type=F32)
        return get

    def get_a(slot):
        def get(part):
            return jnp.dot(rows_of(slot, wrap(y + part)), w[:, :COLS], preferred_element_type=F32)
        return get

    def role_z(slot):
        return wrap(x + slot - z + 4)

    def slot_z(role):
        return wrap(z + role - x + 4)

    ring_b = [RingSum(net, get_b(k), yp, ym, bufs_b, k, 128) for k in range(4)]
    sum_a = BlockSum(net, role_z, slot_z, zp, zm, (*bufs_a, None), 4, 128)
    sum_b = BlockSum(net, role_z, slot_z, zp, zm, (*bufs_b2, keep_b), 1, 128)
    ring_a2 = RingSum(net, sum_a.finish, yp, ym, bufs_a2, 0, 128)

    own_in.wait()
    prep(0, c)
    for copy in w_in:
        copy.wait()
    c_sib.wait_recv()
    prep(0, 1 - c)
    ring_b[0].start()
    sum_a.block(0, get_a(0))
    c_1a.wait_recv()
    c_r1 = net.send(act.at[3, c, top], act.at[2, c, top], me.at_x(1))
    c_2a.wait_recv()
    c_r2 = net.send(act.at[1, c, low], act.at[2, c, low], me.at_x(-1))
    ring_b[0].mid()
    c_1b.wait_recv()
    c_s3 = net.send(act.at[3, c], act.at[3, c], me.sibling)
    c_2b.wait_recv()
    c_s1 = net.send(act.at[1, c], act.at[1, c], me.sibling)
    prep(3, c)
    prep(1, c)
    c_s3.wait_recv()
    prep(3, 1 - c)
    ring_b[3].start()
    sum_a.block(3, get_a(3))
    c_s1.wait_recv()
    prep(1, 1 - c)
    ring_b[1].start()
    sum_a.block(1, get_a(1))
    k_in, v_in = fetch(k_h.at[0], kv), fetch(v_h.at[0], vv)
    wo_in = fetch(wo_h, wo)
    sum_a.mid(0)
    sum_b.block(0, lambda j: ring_b[0].finish())
    c_r1.wait_recv()
    c_r2.wait_recv()
    c_s2 = net.send(act.at[2, c], act.at[2, c], me.sibling)
    prep(2, c)
    ring_b[3].mid()
    ring_b[1].mid()
    c_s2.wait_recv()
    prep(2, 1 - c)
    ring_b[2].start()
    sum_a.block(2, get_a(2))
    sum_a.mid(3)
    sum_a.mid(1)
    sq1 = [
        net.send(sqall.at[wrap(y + step)], sqr1.at[step - 1], me.at_y(step)) for step in range(1, 4)
    ]
    sum_b.block(3, lambda j: ring_b[3].finish())
    sum_b.block(1, lambda j: ring_b[1].finish())
    sum_b.mid(0)
    ring_b[2].mid()
    sum_a.mid(2)
    for copy in sq1:
        copy.wait_recv()
    sqs[...] = (sqall[y] + sqr1[0]) + (sqr1[1] + sqr1[2])
    sq2 = [net.send(sqs, sqr2.at[step - 1], me.at_z(step)) for step in range(1, 4)]
    sum_b.mid(3)
    sum_b.mid(1)
    sum_b.block(2, lambda j: ring_b[2].finish())
    ring_a2.start()
    for copy in sq2:
        copy.wait_recv()
    sqr1[0] = (sqs[...] + sqr2[0]) + (sqr2[1] + sqr2[2])
    own_sq = sqr1[0, pl.ds(z, 1), :]
    inverse = jnp.transpose(jnp.broadcast_to(lax.rsqrt(own_sq / D + 1e-05), (128, 128)))
    tab_in.wait()
    for copy in c_tab:
        copy.wait_recv()
    both = tab[...].reshape(128, 128)
    turned = pltpu.roll(both, 64, 1)
    first = lax.broadcasted_iota(jnp.int32, (128, 128), 1) < 64
    cosine = jnp.where(first, both, turned)
    sine = jnp.where(first, -turned, both)
    slots = lax.broadcasted_iota(jnp.int32, (8, CTX), 1)
    bias[...] = jnp.where(slots < len_ref[0], 0.0, -1e30)
    sum_b.mid(2)
    ring_a2.mid()

    def put(part, col, block):
        sendq[part, :, :, pl.ds(col, 128)] = block.astype(BF).reshape(8, 16, 128)

    def rotated(block):
        block = block * inverse
        return block * cosine + pltpu.roll(block, 64, 1) * sine

    def pass_on(part):
        recvq[part, gy] = sendq[part, gy]
        return [
            net.send(sendq.at[part, wrap(gy + step, 8)], recvq.at[part, gy], me.at_gy(step))
            for step in range(1, 8)
        ]

    fin = sum_b.finish(0)
    for head in range(4):
        put(1, head * 128, rotated(fin[:, head * 128 : (head + 1) * 128]))
    put(1, 512, fin[:, 512:640] * inverse)
    pass_b = pass_on(1)
    fin = ring_a2.finish()
    for head in range(5):
        put(0, head * 128, rotated(fin[:, head * 128 : (head + 1) * 128]))
    pass_a = pass_on(0)

    scale = HD ** (-0.5) * 1.4426950408889634
    contract = (((1,), (1,)), ((), ()))
    token = lax.rem(lax.broadcasted_iota(jnp.int32, (128, 16), 0), 16)
    causal = lax.broadcasted_iota(jnp.int32, (128, 16), 1) <= token
    spot = pl.ds(pl.multiple_of(lax.rem(gy, 4) * 16, 16), 16)
    home = g.at[lax.div(gy, 4), 0, 0, spot]
    k_in.wait()
    v_in.wait()

    def attend(group):
        left, right = recvq[0, group], recvq[1, group]
        query = jnp.concatenate(
            [left[:, h * 128 : (h + 1) * 128] for h in range(4)]
            + [right[:, h * 128 : (h + 1) * 128] for h in range(4)],
            axis=0,
        )
        lanes = pl.ds(pl.multiple_of(group * 128, 128), 128)
        new = lax.dot_general(query, left[:, 512:640], contract, preferred_element_type=F32)
        new = jnp.where(causal, new, -1e30)
        peak = jnp.full((128, CHUNK), -1e30, F32)
        for at in range(0, CTX, CHUNK):
            old = lax.dot_general(
                query, kv[pl.ds(at, CHUNK), lanes], contract, preferred_element_type=F32
            )
            old = (old.reshape(16, 8, CHUNK) + bias[:, pl.ds(at, CHUNK)]).reshape(128, CHUNK)
            score[:, pl.ds(at, CHUNK)] = old
            peak = jnp.maximum(peak, old)
        highest = jnp.maximum(
            jnp.max(peak, axis=1, keepdims=True), jnp.max(new, axis=1, keepdims=True)
        )
        new = jnp.exp2((new - highest) * scale)
        blend = jnp.dot(new.astype(BF), right[:, 512:640], preferred_element_type=F32)
        sums = jnp.zeros((128, CHUNK), F32)
        for at in range(0, CTX, CHUNK):
            old = jnp.exp2((score[:, pl.ds(at, CHUNK)] - highest) * scale)
            sums = sums + old
            blend = blend + jnp.dot(
                old.astype(BF), vv[pl.ds(at, CHUNK), lanes], preferred_element_type=F32
            )
        total = jnp.sum(sums, axis=1, keepdims=True) + jnp.sum(new, axis=1, keepdims=True)
        result = (blend / total).astype(BF)
        return jnp.concatenate([result[h * 16 : (h + 1) * 16] for h in range(8)], axis=1)

    home[...] = attend(gy)
    swap = []
    for step in range(1, 8):
        pass_a[step - 1].wait_recv()
        pass_b[step - 1].wait_recv()
        att[step] = attend(wrap(gy - step + 8, 8))
        swap.append(net.send(att.at[step], home, me.at_gy(-step)))

    a1 = RingCast(net, [g.at[0, k, 0] for k in range(4)], zp, zm)
    b1 = RingCast(net, [g.at[1, 0, k] for k in range(4)], yp, ym)
    a2 = [RingCast(net, [g.at[0, j, k] for k in range(4)], yp, ym) for j in range(4)]
    b2 = [RingCast(net, [g.at[1, k, j] for k in range(4)], zp, zm) for j in range(4)]
    mine = [lax.div(wrap(y + dy), 2) == c for dy in range(4)]
    pair = [net.make(sib_send.at[dy], sib_recv.at[dy], me.sibling, False) for dy in range(4)]

    def get_x(dy):
        def get(role):
            return sib_send[dy, role].astype(F32) + sib_recv[dy, role].astype(F32)
        return get

    ring_x = [
        RingSum(net, get_x(dy), me.at_x(1), me.at_x(-1), bufs_x, dy, 128, False) for dy in range(4)
    ]

    def multiply(dy):
        for half in range(2):
            rows = jnp.concatenate(
                [g[half, wrap(x + role - z + 4), dy] for role in range(4)], axis=0
            )
            term = jnp.dot(rows, wo[...], preferred_element_type=F32).astype(BF)
            for role in range(4):
                sib_send[dy, role, pl.ds(half * 64, 64), :] = term[role * 64 : (role + 1) * 64]

        @pl.when(jnp.logical_not(mine[dy]))
        def _():
            pair[dy].start()

    def sum_start(dy):
        @pl.when(mine[dy])
        def _():
            pair[dy].wait_recv()
            ring_x[dy].start()

    def sum_mid(dy):
        @pl.when(mine[dy])
        def _():
            ring_x[dy].mid()

    def sum_finish(dy):
        @pl.when(mine[dy])
        def _():
            rows = pl.ds(pl.multiple_of(lax.rem(wrap(y + dy), 2) * 128, 128), 128)
            out_ref[rows, :] = ring_x[dy].finish().astype(BF)
            for copy in ring_x[dy].copies:
                copy.wait_send()

        @pl.when(jnp.logical_not(mine[dy]))
        def _():
            pair[dy].wait_send()

    for copy in swap:
        copy.wait_recv()
    a1.start()
    b1.start()
    a2[0].start()
    b2[0].start()
    a1.relay()
    b1.relay()
    a1.near()
    b1.near()
    b2[0].relay()
    a2[1].start()
    a2[3].start()
    b2[1].start()
    b2[3].start()
    a1.far()
    a2[2].start()
    b1.far()
    b2[1].relay()
    b2[3].relay()
    a2[0].relay()
    b2[2].start()
    wo_in.wait()
    b2[0].near()
    b2[0].far()
    multiply(0)
    a2[1].relay()
    a2[3].relay()
    b2[2].relay()
    a2[2].relay()
    sum_start(0)
    for ring in a2:
        ring.near()
    b2[1].near()
    b2[1].far()
    multiply(1)
    sum_mid(0)
    b2[3].near()
    b2[3].far()
    sum_start(1)
    multiply(3)
    sum_start(3)
    sum_mid(1)
    for ring in a2:
        ring.far()
    b2[2].near()
    b2[2].far()
    multiply(2)
    sum_mid(3)
    sum_start(2)
    sum_finish(0)
    sum_finish(1)
    sum_finish(3)
    sum_mid(2)
    sum_finish(2)
    net.drain()
    assert net.count == COPIES, net.count
    assert len(local) == 9


def layer(act, gain, wq, wk, wv, wo, tab, lengths, key_cache, value_cache):
    hbm = pl.BlockSpec(memory_space=pl.ANY)
    vmem = pl.BlockSpec(memory_space=pltpu.VMEM)
    smem = pl.BlockSpec(memory_space=pltpu.SMEM)
    return pl.pallas_call(
        layer_kernel,
        out_shape=jax.ShapeDtypeStruct((256, 512), BF),
        in_specs=[hbm, vmem, hbm, hbm, hbm, hbm, hbm, smem, hbm, hbm],
        out_specs=vmem,
        scratch_shapes=[
            pltpu.VMEM((4, 2, 256, 512), BF),
            pltpu.VMEM((4, 2, 256, 512), BF),
            pltpu.VMEM((512, 1280), BF),
            pltpu.VMEM((8, 16, 128), F32),
            pltpu.VMEM((4, 8, 128), F32),
            pltpu.VMEM((3, 8, 128), F32),
            pltpu.VMEM((8, 128), F32),
            pltpu.VMEM((3, 8, 128), F32),
            pltpu.VMEM((2, 8, 16, COLS), BF),
            pltpu.VMEM((2, 8, 16, COLS), BF),
            pltpu.VMEM((CTX, 1024), BF),
            pltpu.VMEM((CTX, 1024), BF),
            pltpu.VMEM((8, CTX), F32),
            pltpu.VMEM((128, CTX), F32),
            pltpu.VMEM((8, 16, 1024), BF),
            pltpu.VMEM((2, 4, 4, 64, 1024), BF),
            pltpu.VMEM((1024, 512), BF),
            pltpu.VMEM((4, 4, 128, 512), BF),
            pltpu.VMEM((4, 4, 128, 512), BF),
            pltpu.VMEM((4, 1, 128, COLS), F32),
            *block_scratch(4, 128, COLS),
            *block_scratch(1, 128, COLS),
            *ring_scratch(4, 128, COLS),
            *ring_scratch(1, 128, COLS),
            *ring_scratch(4, 128, 512),
            pltpu.SemaphoreType.DMA((COPIES,)),
            pltpu.SemaphoreType.DMA((COPIES,)),
            pltpu.SemaphoreType.DMA((9,)),
        ],
        compiler_params=pltpu.CompilerParams(
            collective_id=0, has_side_effects=True, vmem_limit_bytes=60 * 1024 * 1024
        ),
        name="layer",
    )(act, gain, wq, wk, wv, wo, tab, lengths, key_cache, value_cache)


def places_table(position):
    frequency = jnp.exp(
        jnp.arange(64, dtype=F32) * (-2.0 * math.log(500000.0) / HD)
    )
    places = position + jnp.arange(DRAFT, dtype=jnp.int32)
    angles = places.astype(F32)[:, None] * frequency
    return jnp.concatenate([jnp.cos(angles), jnp.sin(angles)], axis=-1)


def shards(act, gain, wq, wk, wv, wo, key_cache, value_cache, lengths, positions):
    out = layer(
        act.reshape(256, 512), gain.reshape(1, 512), wq, wk, wv, wo,
        places_table(positions), lengths, key_cache, value_cache,
    )
    return out.reshape(16, DRAFT, 512)


def solution(mesh):
    return jax.shard_map(
        shards,
        mesh=mesh,
        in_specs=(
            P("gy", None, "gx"),
            P("gx"),
            P("gx", "gy"),
            P("gx", "gy"),
            P("gx", "gy"),
            P("gy", "gx"),
            P(("gx", "gy"), None, None),
            P(("gx", "gy"), None, None),
            P(("gx", "gy")),
            P(("gx", "gy")),
        ),
        out_specs=P("gy", None, "gx"),
        check_vma=False,
    )
```

```python
import jax
import jax.numpy as jnp
import numpy as np
from jax import lax
from jax.experimental import pallas as pl
from jax.experimental.pallas import tpu as pltpu
from jax.sharding import PartitionSpec as P

D = 8192
HD = 128
KV = 8
CTX = 4096
DRAFT = 16
MESH = pl.DeviceIdType.MESH
F32 = jnp.float32
BF = jnp.bfloat16


def wrap(value, size=4):
    return lax.rem(value + size, size)


class Place:
    def __init__(self):
        gx, gy = lax.axis_index("gx"), lax.axis_index("gy")
        self.gx, self.gy = gx, gy
        self.z, self.y = lax.div(gx, 4), lax.rem(gx, 4)
        self.x, self.c = lax.div(gy, 2), lax.rem(gy, 2)
        self.sibling = (gx, gy + 1 - 2 * self.c)

    def at_x(self, step):
        return (self.gx, wrap(self.x + step) * 2 + self.c)

    def at_y(self, step):
        return (self.z * 4 + wrap(self.y + step), self.gy)

    def at_z(self, step):
        return (wrap(self.z + step) * 4 + self.y, self.gy)

    def at_gy(self, step):
        return (self.gx, wrap(self.gy + step, 8))


class Net:
    def __init__(self, send_sem, recv_sem):
        self.send_sem, self.recv_sem = send_sem, recv_sem
        self.count = 0
        self.sent = []

    def make(self, src, dst, device, drained=True):
        copy = pltpu.make_async_remote_copy(
            src_ref=src,
            dst_ref=dst,
            send_sem=self.send_sem.at[self.count],
            recv_sem=self.recv_sem.at[self.count],
            device_id=device,
            device_id_type=MESH,
        )
        self.count += 1
        if drained:
            self.sent.append(copy)
        return copy

    def send(self, src, dst, device):
        copy = self.make(src, dst, device)
        copy.start()
        return copy

    def drain(self):
        for copy in self.sent:
            copy.wait_send()


def greet(devices):
    barrier = pltpu.get_barrier_semaphore()
    for device in devices:
        pl.semaphore_signal(barrier, inc=1, device_id=device, device_id_type=MESH)
    pl.semaphore_wait(barrier, len(devices))


class RingSum:
    def __init__(self, net, get, plus, minus, bufs, lead, rows, drained=True):
        self.get = get
        self.rows, self.half = rows, rows // 2
        self.so, self.sp, self.sm, self.rom, self.rop, self.rdm, self.rdp, self.kp, self.km = [
            buf.at[lead] for buf in bufs
        ]
        lo, hi = pl.ds(0, self.half), pl.ds(self.half, self.half)
        self.lo, self.hi = lo, hi
        self.om = net.make(self.so.at[lo], self.rom, plus, drained)
        self.op = net.make(self.so.at[hi], self.rop, minus, drained)
        self.m1 = net.make(self.sp.at[hi], self.rdm.at[hi], plus, drained)
        self.p1 = net.make(self.sm.at[lo], self.rdp.at[lo], minus, drained)
        self.m2 = net.make(self.sp.at[lo], self.rdm.at[lo], plus, drained)
        self.p2 = net.make(self.sm.at[hi], self.rdp.at[hi], minus, drained)
        self.copies = [self.om, self.op, self.m1, self.p1, self.m2, self.p2]

    def start_far(self):
        self.so[...] = self.get(2).astype(BF)
        self.om.start()
        self.op.start()

    def start_near(self):
        h = self.half
        part = self.get(1)
        self.kp[...] = part[:h]
        self.sp[self.hi] = part[h:].astype(BF)
        self.m1.start()
        part = self.get(3)
        self.km[...] = part[h:]
        self.sm[self.lo] = part[:h].astype(BF)
        self.p1.start()

    def mid(self):
        self.om.wait_recv()
        self.sp[self.lo] = (self.kp[...] + self.rom[...].astype(F32)).astype(BF)
        self.m2.start()
        self.op.wait_recv()
        self.sm[self.hi] = (self.km[...] + self.rop[...].astype(F32)).astype(BF)
        self.p2.start()

    def finish(self):
        own = self.get(0)
        for copy in (self.m1, self.p1, self.m2, self.p2):
            copy.wait_recv()
        return own + self.rdm[...].astype(F32) + self.rdp[...].astype(F32)


class DirectSum:
    def __init__(self, net, sources, devices, landing, drained=True):
        self.landing = landing
        self.copies = [
            net.make(src, landing.at[i], device, drained)
            for i, (src, device) in enumerate(zip(sources, devices))
        ]

    def finish(self, own):
        for copy in self.copies:
            copy.wait_recv()
        a, b, c = (self.landing[i].astype(F32) for i in range(3))
        return (own + a) + (b + c)


def ring_scratch(count, rows, cols):
    h = rows // 2
    return [
        pltpu.VMEM((count, rows, cols), BF),
        pltpu.VMEM((count, rows, cols), BF),
        pltpu.VMEM((count, rows, cols), BF),
        pltpu.VMEM((count, h, cols), BF),
        pltpu.VMEM((count, h, cols), BF),
        pltpu.VMEM((count, rows, cols), BF),
        pltpu.VMEM((count, rows, cols), BF),
        pltpu.VMEM((count, h, cols), F32),
        pltpu.VMEM((count, h, cols), F32),
    ]


class BlockSum:
    def __init__(self, net, role, slot, plus, minus, bufs, rows):
        self.role, self.slot = role, slot
        self.out, self.rom, self.rop, self.rdm, self.rdp = bufs
        h = rows // 2
        lo, hi = pl.ds(0, h), pl.ds(h, h)
        self.lo, self.hi = lo, hi
        far, near, last = slot(2), slot(1), slot(3)
        self.om = net.make(self.out.at[far, :, lo], self.rom, plus)
        self.op = net.make(self.out.at[far, :, hi], self.rop, minus)
        self.m1 = net.make(self.out.at[near, :, hi], self.rdm.at[:, hi], plus)
        self.p1 = net.make(self.out.at[last, :, lo], self.rdp.at[:, lo], minus)
        self.m2 = net.make(self.out.at[near, :, lo], self.rdm.at[:, lo], plus)
        self.p2 = net.make(self.out.at[last, :, hi], self.rdp.at[:, hi], minus)

    def block(self, k):
        role = self.role(k)

        @pl.when(role == 2)
        def _():
            self.om.start()
            self.op.start()

        @pl.when(role == 1)
        def _():
            self.m1.start()

        @pl.when(role == 3)
        def _():
            self.p1.start()

    def mid(self, k):
        role = self.role(k)

        @pl.when(role == 1)
        def _():
            self.om.wait_recv()
            total = self.out[k, :, self.lo].astype(F32) + self.rom[...].astype(F32)
            self.out[k, :, self.lo] = total.astype(BF)
            self.m2.start()

        @pl.when(role == 3)
        def _():
            self.op.wait_recv()
            total = self.out[k, :, self.hi].astype(F32) + self.rop[...].astype(F32)
            self.out[k, :, self.hi] = total.astype(BF)
            self.p2.start()

    def arrived(self):
        for copy in (self.m1, self.p1, self.m2, self.p2):
            copy.wait_recv()

    def finish(self, j):
        own = self.out[self.slot(0), j].astype(F32)
        return own + self.rdm[j].astype(F32) + self.rdp[j].astype(F32)


def block_scratch(parts, rows, cols):
    return [
        pltpu.VMEM((4, parts, rows, cols), BF),
        pltpu.VMEM((parts, rows // 2, cols), BF),
        pltpu.VMEM((parts, rows // 2, cols), BF),
        pltpu.VMEM((parts, rows, cols), BF),
        pltpu.VMEM((parts, rows, cols), BF),
    ]


class RingCast:
    def __init__(self, net, slots, plus, minus):
        lo, hi = pl.ds(0, 32), pl.ds(32, 32)
        own, next_, far, last = slots
        self.to_plus = net.make(own, last, plus)
        self.to_minus = net.make(own, next_, minus)
        self.on_plus = net.make(last.at[lo], far.at[lo], plus)
        self.on_minus = net.make(next_.at[hi], far.at[hi], minus)

    def start(self):
        self.to_plus.start()
        self.to_minus.start()

    def relay(self):
        self.to_plus.wait_recv()
        self.on_plus.start()
        self.to_minus.wait_recv()
        self.on_minus.start()

    def far(self):
        self.on_plus.wait_recv()
        self.on_minus.wait_recv()


COLS = 640
COPIES = 198
CHUNK = 1024


def layer_kernel(
    act_h, gain_ref, wq_h, wk_h, wv_h, wo_h, freq_ref, pos_ref, len_ref, k_h, v_h, out_ref,
    act, scaled, w, prod, tab, sqall, sqr1, sqs, sqr2, sendq, recvq, kv, vv, bias, score, att,
    g, wo, sib_send, sib_recv, keep_b, *rest,
):
    bufs_a = [rest[:5], rest[5:10]]
    bufs_b = [rest[10:19], rest[19:28]]
    out_b, in_b, out_a2, in_a2, out_x, in_x, send_sem, recv_sem, local_sem = rest[28:]
    me = Place()
    x, c, y, z, gy = me.x, me.c, me.y, me.z, me.gy
    net = Net(send_sem, recv_sem)
    ym, yp, zm, zp = me.at_y(-1), me.at_y(1), me.at_z(-1), me.at_z(1)

    local = []

    def fetch(src, dst):
        copy = pltpu.make_async_copy(src, dst, local_sem.at[len(local)])
        copy.start()
        local.append(copy)
        return copy

    own_in = fetch(act_h, act.at[0, c])
    w_in = [
        fetch(wq_h.at[:, pl.ds(0, 512)], w.at[:, pl.ds(0, 512)]),
        fetch(wk_h, w.at[:, pl.ds(512, 128)]),
        fetch(wq_h.at[:, pl.ds(512, 512)], w.at[:, pl.ds(640, 512)]),
        fetch(wv_h, w.at[:, pl.ds(1152, 128)]),
    ]
    token = lax.broadcasted_iota(jnp.int32, (DRAFT, HD), 0)
    angles = (pos_ref[0] + token).astype(F32) * freq_ref[...]
    half = lax.broadcasted_iota(jnp.int32, (DRAFT, HD), 1) < HD // 2
    tab[gy] = jnp.where(half, jnp.cos(angles), jnp.sin(angles))

    greet(
        [me.at_gy(step) for step in range(1, 8)]
        + [me.at_y(step) for step in range(1, 4)]
        + [me.at_z(step) for step in range(1, 4)]
    )

    span = (pl.ds(0, 64), pl.ds(64, 64))
    c_sib, c_pj, c_mj, c_rp, c_rm, c_s = [], [], [], [], [], [{}, {}]

    def to_neighbours(h):
        c_pj.append([None, None])
        c_mj.append([None, None])
        for j in range(2):
            src = act_h.at[j, span[h]]
            c_pj[h][j] = net.send(src, act.at[3, c, j, span[h]], me.at_x(1))
            src = act_h.at[1 - j, span[h]]
            c_mj[h][1 - j] = net.send(src, act.at[1, c, 1 - j, span[h]], me.at_x(-1))

    def to_sibling(slot, h):
        part = act.at[slot, c, :, span[h]]
        c_s[h][slot] = net.send(part, part, me.sibling)

    def relay(h):
        c_pj[h][0].wait_recv()
        c_rp.append(net.send(act.at[3, c, 0, span[h]], act.at[2, c, 0, span[h]], me.at_x(1)))
        c_mj[h][1].wait_recv()
        c_rm.append(net.send(act.at[1, c, 1, span[h]], act.at[2, c, 1, span[h]], me.at_x(-1)))

    def near(h):
        c_pj[h][1].wait_recv()
        to_sibling(3, h)
        c_mj[h][0].wait_recv()
        to_sibling(1, h)

    def far(h):
        c_rp[h].wait_recv()
        c_rm[h].wait_recv()
        to_sibling(2, h)

    for h in range(2):
        c_sib.append(net.send(act_h.at[:, span[h]], act.at[0, c, :, span[h]], me.sibling))
    to_neighbours(0)
    c_tab = [net.send(tab.at[gy], tab.at[gy], me.at_gy(step)) for step in range(1, 8)]

    gain = gain_ref[...].astype(F32).reshape(1, 512)

    def prep(slot, core, h):
        for j in range(2):
            wide = act[slot, core, j, span[h], :].astype(F32)
            scaled[slot, h, 2 * core + j] = (wide * gain).astype(BF)
            square = wide * wide
            fold = (square[:, 0:128] + square[:, 128:256]) + (square[:, 256:384] + square[:, 384:512])
            row = jnp.sum(jnp.transpose(fold), axis=0, keepdims=True)
            sqall[h, 2 * core + j, pl.ds(wrap(x + slot), 1), pl.ds(0, 64)] = row

    def get_b(slot, h):
        def get(role):
            return prod[h, slot, wrap(y + role)]
        return get

    def role_z(slot):
        return wrap(x + slot - z + 4)

    def slot_z(role):
        return wrap(z + role - x + 4)

    ring_b = [
        [RingSum(net, get_b(k, h), yp, ym, bufs_b[h], k, 64) for k in range(4)] for h in range(2)
    ]
    sum_a = [BlockSum(net, role_z, slot_z, zp, zm, bufs_a[h], 64) for h in range(2)]
    sum_b = [
        DirectSum(
            net, [out_b.at[h, slot_z(r)] for r in (1, 2, 3)], [me.at_z(r) for r in (1, 2, 3)],
            in_b.at[h],
        )
        for h in range(2)
    ]
    sum_a2 = [
        DirectSum(
            net, [out_a2.at[h, r - 1] for r in (1, 2, 3)], [me.at_y(r) for r in (1, 2, 3)],
            in_a2.at[h],
        )
        for h in range(2)
    ]

    def multiply_in(k, h):
        rows = scaled[k, h].reshape(256, 512)
        term = jnp.dot(rows, w[:, COLS:], preferred_element_type=F32)
        for j in range(4):
            prod[h, k, j] = term[j * 64 : (j + 1) * 64]
        ring_b[h][k].start_far()
        term = jnp.dot(rows, w[:, :COLS], preferred_element_type=F32).astype(BF)
        for j in range(4):
            sum_a[h].out[k, wrap(j - y)] = term[j * 64 : (j + 1) * 64]
        sum_a[h].block(k)
        ring_b[h][k].start_near()

    def block_b(slot, h):
        value = ring_b[h][slot].finish()
        keep_b[h, slot] = value
        out_b[h, slot] = value.astype(BF)
        for r in (1, 2, 3):

            @pl.when(role_z(slot) == r)
            def _():
                sum_b[h].copies[r - 1].start()

    def part_a2(h):
        sum_a[h].arrived()
        for r in (2, 1, 3):
            out_a2[h, r - 1] = sum_a[h].finish(r).astype(BF)
            sum_a2[h].copies[r - 1].start()

    own_in.wait()
    prep(0, c, 0)
    for copy in w_in:
        copy.wait()
    c_sib[0].wait_recv()
    prep(0, 1 - c, 0)
    multiply_in(0, 0)
    relay(0)
    to_neighbours(1)
    prep(0, c, 1)
    c_sib[1].wait_recv()
    prep(0, 1 - c, 1)
    multiply_in(0, 1)
    near(0)
    ring_b[0][0].mid()
    prep(3, c, 0)
    prep(1, c, 0)
    c_s[0][3].wait_recv()
    prep(3, 1 - c, 0)
    multiply_in(3, 0)
    c_s[0][1].wait_recv()
    prep(1, 1 - c, 0)
    multiply_in(1, 0)
    far(0)
    relay(1)
    prep(2, c, 0)
    c_s[0][2].wait_recv()
    prep(2, 1 - c, 0)
    multiply_in(2, 0)
    near(1)
    sum_a[0].mid(0)
    ring_b[1][0].mid()
    ring_b[0][3].mid()
    ring_b[0][1].mid()
    block_b(0, 0)
    prep(3, c, 1)
    prep(1, c, 1)
    c_s[1][3].wait_recv()
    prep(3, 1 - c, 1)
    multiply_in(3, 1)
    c_s[1][1].wait_recv()
    prep(1, 1 - c, 1)
    multiply_in(1, 1)
    far(1)
    sum_a[0].mid(3)
    sum_a[0].mid(1)
    ring_b[0][2].mid()
    prep(2, c, 1)
    c_s[1][2].wait_recv()
    prep(2, 1 - c, 1)
    multiply_in(2, 1)
    k_in, v_in = fetch(k_h.at[0], kv), fetch(v_h.at[0], vv)
    wo_in = fetch(wo_h, wo)
    sq1 = [
        net.send(sqall.at[:, wrap(y + step)], sqr1.at[step - 1], me.at_y(step))
        for step in range(1, 4)
    ]
    block_b(3, 0)
    block_b(1, 0)
    sum_a[0].mid(2)
    sum_a[1].mid(0)
    block_b(0, 1)
    ring_b[1][3].mid()
    ring_b[1][1].mid()
    block_b(2, 0)
    sum_a[1].mid(3)
    sum_a[1].mid(1)
    ring_b[1][2].mid()
    for copy in sq1:
        copy.wait_recv()
    sqs[...] = (sqall[:, y] + sqr1[0]) + (sqr1[1] + sqr1[2])
    sq2 = [net.send(sqs, sqr2.at[step - 1], me.at_z(step)) for step in range(1, 4)]
    part_a2(0)
    sum_a[1].mid(2)
    block_b(3, 1)
    block_b(1, 1)
    block_b(2, 1)
    part_a2(1)
    for copy in sq2:
        copy.wait_recv()
    sqr1[0] = (sqs[...] + sqr2[0]) + (sqr2[1] + sqr2[2])
    halves = [
        jnp.transpose(
            jnp.broadcast_to(lax.rsqrt(sqr1[0, h, pl.ds(z, 1), :] / D + 1e-05), (128, 128))
        )[:64]
        for h in range(2)
    ]
    for copy in c_tab:
        copy.wait_recv()
    inverse = jnp.concatenate(halves, axis=0)
    both = tab[...].reshape(128, 128)
    turned = pltpu.roll(both, 64, 1)
    first = lax.broadcasted_iota(jnp.int32, (128, 128), 1) < 64
    cosine = jnp.where(first, both, turned)
    sine = jnp.where(first, -turned, both)
    slots = lax.broadcasted_iota(jnp.int32, (8, CTX), 1)
    bias[...] = jnp.where(slots < len_ref[0], 0.0, -1e30)

    def put(part, col, block):
        sendq[part, :, :, pl.ds(col, 128)] = block.astype(BF).reshape(8, 16, 128)

    def rotated(block):
        block = block * inverse
        return block * cosine + pltpu.roll(block, 64, 1) * sine

    partners = []
    for xx, cc in (
        (x, 1 - c),
        (x + 1 - 2 * lax.rem(x, 2), c),
        (3 - x, c),
        (wrap(x + 2), c),
        (wrap(x + 2), 1 - c),
        (x + 1 - 2 * lax.rem(x, 2), 1 - c),
        (3 - x, 1 - c),
    ):
        partners.append(xx * 2 + cc)

    def pass_on(part):
        recvq[part, gy] = sendq[part, gy]
        return [
            net.send(sendq.at[part, other], recvq.at[part, gy], (me.gx, other))
            for other in partners
        ]

    fin = jnp.concatenate([sum_b[h].finish(keep_b[h, slot_z(0)]) for h in range(2)], axis=0)
    for head in range(4):
        put(1, head * 128, rotated(fin[:, head * 128 : (head + 1) * 128]))
    put(1, 512, fin[:, 512:640] * inverse)
    pass_b = pass_on(1)
    fin = jnp.concatenate([sum_a2[h].finish(sum_a[h].finish(0)) for h in range(2)], axis=0)
    for head in range(5):
        put(0, head * 128, rotated(fin[:, head * 128 : (head + 1) * 128]))
    pass_a = pass_on(0)

    scale = HD ** (-0.5) * 1.4426950408889634
    contract = (((1,), (1,)), ((), ()))
    draft = lax.rem(lax.broadcasted_iota(jnp.int32, (128, 16), 0), 16)
    causal = lax.broadcasted_iota(jnp.int32, (128, 16), 1) <= draft
    spot = pl.ds(pl.multiple_of(lax.rem(gy, 4) * 16, 16), 16)
    home = g.at[lax.div(gy, 4), 0, 0, spot]
    k_in.wait()
    v_in.wait()

    def attend(group):
        left, right = recvq[0, group], recvq[1, group]
        query = jnp.concatenate(
            [left[:, h * 128 : (h + 1) * 128] for h in range(4)]
            + [right[:, h * 128 : (h + 1) * 128] for h in range(4)],
            axis=0,
        )
        lanes = pl.ds(pl.multiple_of(group * 128, 128), 128)
        new = lax.dot_general(query, left[:, 512:640], contract, preferred_element_type=F32)
        new = jnp.where(causal, new, -1e30)
        peak = jnp.full((128, CHUNK), -1e30, F32)
        for at in range(0, CTX, CHUNK):
            old = lax.dot_general(
                query, kv[pl.ds(at, CHUNK), lanes], contract, preferred_element_type=F32
            )
            old = (old.reshape(16, 8, CHUNK) + bias[:, pl.ds(at, CHUNK)]).reshape(128, CHUNK)
            score[:, pl.ds(at, CHUNK)] = old
            peak = jnp.maximum(peak, old)
        highest = jnp.maximum(
            jnp.max(peak, axis=1, keepdims=True), jnp.max(new, axis=1, keepdims=True)
        )
        new = jnp.exp2((new - highest) * scale)
        blend = jnp.dot(new.astype(BF), right[:, 512:640], preferred_element_type=F32)
        sums = jnp.zeros((128, CHUNK), F32)
        for at in range(0, CTX, CHUNK):
            old = jnp.exp2((score[:, pl.ds(at, CHUNK)] - highest) * scale)
            sums = sums + old
            blend = blend + jnp.dot(
                old.astype(BF), vv[pl.ds(at, CHUNK), lanes], preferred_element_type=F32
            )
        total = jnp.sum(sums, axis=1, keepdims=True) + jnp.sum(new, axis=1, keepdims=True)
        result = (blend / total).astype(BF)
        return jnp.concatenate([result[h * 16 : (h + 1) * 16] for h in range(8)], axis=1)

    home[...] = attend(gy)
    swap = []
    for step, other in enumerate(partners):
        pass_a[step].wait_recv()
        pass_b[step].wait_recv()
        att[step] = attend(other)
        swap.append(net.send(att.at[step], home, (me.gx, other)))

    a1 = RingCast(net, [g.at[0, k, 0] for k in range(4)], zp, zm)
    b1 = RingCast(net, [g.at[1, 0, k] for k in range(4)], yp, ym)
    a2 = [RingCast(net, [g.at[0, j, k] for k in range(4)], yp, ym) for j in range(4)]
    b2 = [RingCast(net, [g.at[1, k, j] for k in range(4)], zp, zm) for j in range(4)]
    mine = [lax.div(wrap(y + dy), 2) == c for dy in range(4)]
    pair = [
        [
            net.make(sib_send.at[dy, :, part], sib_recv.at[dy, :, part], me.sibling, False)
            for part in span
        ]
        for dy in range(4)
    ]
    sum_x = [
        [
            [
                net.make(out_x.at[dy, r - 1, part], in_x.at[dy, r - 1, part], me.at_x(r), False)
                for r in (1, 2, 3)
            ]
            for part in span
        ]
        for dy in range(4)
    ]

    def both_cores(dy, role, part):
        return sib_send[dy, role, part].astype(F32) + sib_recv[dy, role, part].astype(F32)

    def multiply(half, dy):
        rows = jnp.concatenate(
            [g[half, wrap(x + role - z + 4), dy] for role in range(4)], axis=0
        )
        term = jnp.dot(rows, wo[...], preferred_element_type=F32).astype(BF)
        for role in range(4):
            sib_send[dy, role, span[half], :] = term[role * 64 : (role + 1) * 64]

        @pl.when(jnp.logical_not(mine[dy]))
        def _():
            pair[dy][half].start()

    def sum_start(half, dy):
        @pl.when(mine[dy])
        def _():
            pair[dy][half].wait_recv()
            for r in (2, 1, 3):
                out_x[dy, r - 1, span[half]] = both_cores(dy, r, span[half]).astype(BF)
                sum_x[dy][half][r - 1].start()

    def sum_finish(dy):
        @pl.when(mine[dy])
        def _():
            base = lax.rem(wrap(y + dy), 2) * 128
            for half in range(2):
                for copy in sum_x[dy][half]:
                    copy.wait_recv()
                total = both_cores(dy, 0, span[half])
                for r in range(3):
                    total = total + in_x[dy, r, span[half]].astype(F32)
                rows = pl.ds(pl.multiple_of(base + half * 64, 64), 64)
                out_ref[rows, :] = total.astype(BF)
                for copy in sum_x[dy][half]:
                    copy.wait_send()

        @pl.when(jnp.logical_not(mine[dy]))
        def _():
            for copy in pair[dy]:
                copy.wait_send()

    for copy in swap:
        copy.wait_recv()
    a1.start()
    b1.start()
    a2[0].start()
    b2[0].start()
    a1.relay()
    b1.relay()
    for ring in (a2[1], b2[1], a2[3], b2[3]):
        ring.start()
    a2[0].relay()
    b2[0].relay()
    a1.far()
    b1.far()
    a2[2].start()
    b2[2].start()
    wo_in.wait()
    multiply(0, 0)
    for ring in (a2[1], b2[1], a2[3], b2[3]):
        ring.relay()
    b2[0].far()
    multiply(1, 0)
    sum_start(0, 0)
    a2[2].relay()
    multiply(0, 1)
    multiply(0, 3)
    sum_start(1, 0)
    b2[2].relay()
    b2[1].far()
    multiply(1, 1)
    sum_start(0, 1)
    sum_start(0, 3)
    b2[3].far()
    multiply(1, 3)
    sum_start(1, 1)
    for ring in a2:
        ring.far()
    multiply(0, 2)
    sum_start(1, 3)
    b2[2].far()
    multiply(1, 2)
    sum_start(0, 2)
    sum_start(1, 2)
    sum_finish(0)
    sum_finish(1)
    sum_finish(3)
    sum_finish(2)
    net.drain()
    assert net.count == COPIES, net.count
    assert len(local) == 8


def layer(act, gain, wq, wk, wv, wo, freq, positions, lengths, key_cache, value_cache):
    hbm = pl.BlockSpec(memory_space=pl.ANY)
    vmem = pl.BlockSpec(memory_space=pltpu.VMEM)
    smem = pl.BlockSpec(memory_space=pltpu.SMEM)
    return pl.pallas_call(
        layer_kernel,
        out_shape=jax.ShapeDtypeStruct((256, 512), BF),
        in_specs=[hbm, vmem, hbm, hbm, hbm, hbm, vmem, smem, smem, hbm, hbm],
        out_specs=vmem,
        scratch_shapes=[
            pltpu.VMEM((4, 2, 2, 128, 512), BF),
            pltpu.VMEM((4, 2, 4, 64, 512), BF),
            pltpu.VMEM((512, 1280), BF),
            pltpu.VMEM((2, 4, 4, 64, COLS), F32),
            pltpu.VMEM((8, 16, 128), F32),
            pltpu.VMEM((2, 4, 8, 128), F32),
            pltpu.VMEM((3, 2, 8, 128), F32),
            pltpu.VMEM((2, 8, 128), F32),
            pltpu.VMEM((3, 2, 8, 128), F32),
            pltpu.VMEM((2, 8, 16, COLS), BF),
            pltpu.VMEM((2, 8, 16, COLS), BF),
            pltpu.VMEM((CTX, 1024), BF),
            pltpu.VMEM((CTX, 1024), BF),
            pltpu.VMEM((8, CTX), F32),
            pltpu.VMEM((128, CTX), F32),
            pltpu.VMEM((7, 16, 1024), BF),
            pltpu.VMEM((2, 4, 4, 64, 1024), BF),
            pltpu.VMEM((1024, 512), BF),
            pltpu.VMEM((4, 4, 128, 512), BF),
            pltpu.VMEM((4, 4, 128, 512), BF),
            pltpu.VMEM((2, 4, 64, COLS), F32),
            *block_scratch(4, 64, COLS),
            *block_scratch(4, 64, COLS),
            *ring_scratch(4, 64, COLS),
            *ring_scratch(4, 64, COLS),
            pltpu.VMEM((2, 4, 64, COLS), BF),
            pltpu.VMEM((2, 3, 64, COLS), BF),
            pltpu.VMEM((2, 3, 64, COLS), BF),
            pltpu.VMEM((2, 3, 64, COLS), BF),
            pltpu.VMEM((4, 3, 128, 512), BF),
            pltpu.VMEM((4, 3, 128, 512), BF),
            pltpu.SemaphoreType.DMA((COPIES,)),
            pltpu.SemaphoreType.DMA((COPIES,)),
            pltpu.SemaphoreType.DMA((8,)),
        ],
        compiler_params=pltpu.CompilerParams(
            collective_id=0, has_side_effects=True, vmem_limit_bytes=60 * 1024 * 1024
        ),
        name="layer",
    )(act, gain, wq, wk, wv, wo, freq, positions, lengths, key_cache, value_cache)


def frequencies():
    power = np.arange(64, dtype=np.float64) * (-2.0 / HD)
    row = np.tile(np.power(500000.0, power), 2)
    return jnp.asarray(np.broadcast_to(row, (DRAFT, HD)).astype(np.float32))


def shards(act, gain, wq, wk, wv, wo, key_cache, value_cache, lengths, positions):
    out = layer(
        act.reshape(2, 128, 512), gain, wq, wk, wv, wo,
        frequencies(), positions, lengths, key_cache, value_cache,
    )
    return out.reshape(16, DRAFT, 512)


def solution(mesh):
    return jax.shard_map(
        shards,
        mesh=mesh,
        in_specs=(
            P("gy", None, "gx"),
            P("gx"),
            P("gx", "gy"),
            P("gx", "gy"),
            P("gx", "gy"),
            P("gy", "gx"),
            P(("gx", "gy"), None, None),
            P(("gx", "gy"), None, None),
            P(("gx", "gy")),
            P(("gx", "gy")),
        ),
        out_specs=P("gy", None, "gx"),
        check_vma=False,
    )
```

```python
import jax
import jax.numpy as jnp
import numpy as np
from jax import lax
from jax.experimental import pallas as pl
from jax.experimental.pallas import tpu as pltpu
from jax.sharding import PartitionSpec as P

D = 8192
HD = 128
KV = 8
CTX = 4096
DRAFT = 16
MESH = pl.DeviceIdType.MESH
F32 = jnp.float32
BF = jnp.bfloat16


def wrap(value, size=4):
    return lax.rem(value + size, size)


class Place:
    def __init__(self):
        gx, gy = lax.axis_index("gx"), lax.axis_index("gy")
        self.gx, self.gy = gx, gy
        self.z, self.y = lax.div(gx, 4), lax.rem(gx, 4)
        self.x, self.c = lax.div(gy, 2), lax.rem(gy, 2)
        self.sibling = (gx, gy + 1 - 2 * self.c)

    def at_x(self, step):
        return (self.gx, wrap(self.x + step) * 2 + self.c)

    def at_y(self, step):
        return (self.z * 4 + wrap(self.y + step), self.gy)

    def at_z(self, step):
        return (wrap(self.z + step) * 4 + self.y, self.gy)

    def at_gy(self, step):
        return (self.gx, wrap(self.gy + step, 8))


class Net:
    def __init__(self, send_sem, recv_sem):
        self.send_sem, self.recv_sem = send_sem, recv_sem
        self.count = 0
        self.sent = []

    def make(self, src, dst, device, drained=True):
        copy = pltpu.make_async_remote_copy(
            src_ref=src,
            dst_ref=dst,
            send_sem=self.send_sem.at[self.count],
            recv_sem=self.recv_sem.at[self.count],
            device_id=device,
            device_id_type=MESH,
        )
        self.count += 1
        if drained:
            self.sent.append(copy)
        return copy

    def send(self, src, dst, device):
        copy = self.make(src, dst, device)
        copy.start()
        return copy

    def drain(self):
        for copy in self.sent:
            copy.wait_send()


def greet(devices):
    barrier = pltpu.get_barrier_semaphore()
    for device in devices:
        pl.semaphore_signal(barrier, inc=1, device_id=device, device_id_type=MESH)
    pl.semaphore_wait(barrier, len(devices))


class RingSum:
    def __init__(self, net, get, plus, minus, bufs, lead, rows, drained=True):
        self.get = get
        self.rows, self.half = rows, rows // 2
        self.so, self.sp, self.sm, self.rom, self.rop, self.rdm, self.rdp, self.kp, self.km = [
            buf.at[lead] for buf in bufs
        ]
        lo, hi = pl.ds(0, self.half), pl.ds(self.half, self.half)
        self.lo, self.hi = lo, hi
        self.om = net.make(self.so.at[lo], self.rom, plus, drained)
        self.op = net.make(self.so.at[hi], self.rop, minus, drained)
        self.m1 = net.make(self.sp.at[hi], self.rdm.at[hi], plus, drained)
        self.p1 = net.make(self.sm.at[lo], self.rdp.at[lo], minus, drained)
        self.m2 = net.make(self.sp.at[lo], self.rdm.at[lo], plus, drained)
        self.p2 = net.make(self.sm.at[hi], self.rdp.at[hi], minus, drained)
        self.copies = [self.om, self.op, self.m1, self.p1, self.m2, self.p2]

    def start_far(self):
        self.so[...] = self.get(2).astype(BF)
        self.om.start()
        self.op.start()

    def start_near(self):
        h = self.half
        part = self.get(1)
        self.kp[...] = part[:h]
        self.sp[self.hi] = part[h:].astype(BF)
        self.m1.start()
        part = self.get(3)
        self.km[...] = part[h:]
        self.sm[self.lo] = part[:h].astype(BF)
        self.p1.start()

    def mid(self):
        self.om.wait_recv()
        self.sp[self.lo] = (self.kp[...] + self.rom[...].astype(F32)).astype(BF)
        self.m2.start()
        self.op.wait_recv()
        self.sm[self.hi] = (self.km[...] + self.rop[...].astype(F32)).astype(BF)
        self.p2.start()

    def finish(self):
        own = self.get(0)
        for copy in (self.m1, self.p1, self.m2, self.p2):
            copy.wait_recv()
        return own + self.rdm[...].astype(F32) + self.rdp[...].astype(F32)


class DirectSum:
    def __init__(self, net, sources, devices, landing, drained=True):
        self.landing = landing
        self.copies = [
            net.make(src, landing.at[i], device, drained)
            for i, (src, device) in enumerate(zip(sources, devices))
        ]

    def finish(self, own):
        for copy in self.copies:
            copy.wait_recv()
        a, b, c = (self.landing[i].astype(F32) for i in range(3))
        return (own + a) + (b + c)


def ring_scratch(count, rows, cols):
    h = rows // 2
    return [
        pltpu.VMEM((count, rows, cols), BF),
        pltpu.VMEM((count, rows, cols), BF),
        pltpu.VMEM((count, rows, cols), BF),
        pltpu.VMEM((count, h, cols), BF),
        pltpu.VMEM((count, h, cols), BF),
        pltpu.VMEM((count, rows, cols), BF),
        pltpu.VMEM((count, rows, cols), BF),
        pltpu.VMEM((count, h, cols), F32),
        pltpu.VMEM((count, h, cols), F32),
    ]


class BlockSum:
    def __init__(self, net, role, slot, plus, minus, bufs, parts, rows):
        self.role, self.slot, self.parts = role, slot, parts
        self.out, self.rom, self.rop, self.rdm, self.rdp = bufs
        h = rows // 2
        lo, hi = pl.ds(0, h), pl.ds(h, h)
        self.lo, self.hi = lo, hi
        far, near, last = slot(2), slot(1), slot(3)
        span = range(parts)
        self.om = [net.make(self.out.at[far, j, lo], self.rom.at[j], plus) for j in span]
        self.op = [net.make(self.out.at[far, j, hi], self.rop.at[j], minus) for j in span]
        self.m1 = [net.make(self.out.at[near, j, hi], self.rdm.at[j, hi], plus) for j in span]
        self.p1 = [net.make(self.out.at[last, j, lo], self.rdp.at[j, lo], minus) for j in span]
        self.m2 = [net.make(self.out.at[near, j, lo], self.rdm.at[j, lo], plus) for j in span]
        self.p2 = [net.make(self.out.at[last, j, hi], self.rdp.at[j, hi], minus) for j in span]

    def block(self, k):
        role = self.role(k)

        @pl.when(role == 2)
        def _():
            for j in (2, 1, 3, 0):
                self.om[j].start()
                self.op[j].start()

        @pl.when(role == 1)
        def _():
            for j in (2, 1, 3, 0):
                self.m1[j].start()

        @pl.when(role == 3)
        def _():
            for j in (2, 1, 3, 0):
                self.p1[j].start()

    def value(self, k, j, rows):
        return self.out[k, j, rows].astype(F32)

    def mid(self, k):
        role = self.role(k)
        order = (2, 1, 3, 0)

        @pl.when(role == 1)
        def _():
            for j in order:
                self.om[j].wait_recv()
                total = self.value(k, j, self.lo) + self.rom[j].astype(F32)
                self.out[k, j, self.lo] = total.astype(BF)
                self.m2[j].start()

        @pl.when(role == 3)
        def _():
            for j in order:
                self.op[j].wait_recv()
                total = self.value(k, j, self.hi) + self.rop[j].astype(F32)
                self.out[k, j, self.hi] = total.astype(BF)
                self.p2[j].start()

    def finish(self, j):
        own = self.value(self.slot(0), j, slice(None))
        for copy in (self.m1[j], self.p1[j], self.m2[j], self.p2[j]):
            copy.wait_recv()
        return own + self.rdm[j].astype(F32) + self.rdp[j].astype(F32)


def block_scratch(parts, rows, cols):
    return [
        pltpu.VMEM((4, parts, rows, cols), BF),
        pltpu.VMEM((parts, rows // 2, cols), BF),
        pltpu.VMEM((parts, rows // 2, cols), BF),
        pltpu.VMEM((parts, rows, cols), BF),
        pltpu.VMEM((parts, rows, cols), BF),
    ]


class RingCast:
    def __init__(self, net, slots, plus, minus):
        lo, hi = pl.ds(0, 16), pl.ds(16, 16)
        own, next_, far, last = slots
        self.to_plus = net.make(own, last, plus)
        self.to_minus = net.make(own, next_, minus)
        self.on_plus = net.make(last.at[lo], far.at[lo], plus)
        self.on_minus = net.make(next_.at[hi], far.at[hi], minus)

    def start(self):
        self.to_plus.start()
        self.to_minus.start()

    def relay(self):
        self.to_plus.wait_recv()
        self.on_plus.start()
        self.to_minus.wait_recv()
        self.on_minus.start()

    def far(self):
        self.on_plus.wait_recv()
        self.on_minus.wait_recv()


COLS = 640
COPIES = 274
CHUNK = 1024


def layer_kernel(
    act_h, gain_ref, wq_h, wk_h, wv_h, wo_h, freq_ref, pos_ref, len_ref, k_h, v_h, out_ref,
    act, scaled, w, prod, tab, sqall, sqr1, sqs, sqr2, sendq, recvq, kv, vv, bias, score, att,
    g, wo, sib_send, sib_recv, keep_b, *rest,
):
    bufs_a = [rest[:5], rest[5:10]]
    bufs_b = [rest[10:19], rest[19:28]]
    out_b, in_b, out_a2, in_a2, out_x, in_x, send_sem, recv_sem, local_sem = rest[28:]
    me = Place()
    x, c, y, z, gy = me.x, me.c, me.y, me.z, me.gy
    net = Net(send_sem, recv_sem)
    ym, yp, zm, zp = me.at_y(-1), me.at_y(1), me.at_z(-1), me.at_z(1)

    local = []

    def fetch(src, dst):
        copy = pltpu.make_async_copy(src, dst, local_sem.at[len(local)])
        copy.start()
        local.append(copy)
        return copy

    own_in = fetch(act_h, act.at[0, c])
    w_in = [
        fetch(wq_h.at[:, pl.ds(0, 512)], w.at[:, pl.ds(0, 512)]),
        fetch(wk_h, w.at[:, pl.ds(512, 128)]),
        fetch(wq_h.at[:, pl.ds(512, 512)], w.at[:, pl.ds(640, 512)]),
        fetch(wv_h, w.at[:, pl.ds(1152, 128)]),
    ]
    token = lax.broadcasted_iota(jnp.int32, (DRAFT, HD), 0)
    angles = (pos_ref[0] + token).astype(F32) * freq_ref[...]
    half = lax.broadcasted_iota(jnp.int32, (DRAFT, HD), 1) < HD // 2
    tab[gy] = jnp.where(half, jnp.cos(angles), jnp.sin(angles))

    greet(
        [me.at_gy(step) for step in range(1, 8)]
        + [me.at_y(step) for step in range(1, 4)]
        + [me.at_z(step) for step in range(1, 4)]
    )

    span = (pl.ds(0, 64), pl.ds(64, 64))
    c_sib, c_pj, c_mj, c_rp, c_rm, c_s = [], [], [], [], [], [{}, {}]

    def to_neighbours(h):
        c_pj.append([None, None])
        c_mj.append([None, None])
        for j in range(2):
            src = act_h.at[j, span[h]]
            c_pj[h][j] = net.send(src, act.at[3, c, j, span[h]], me.at_x(1))
            src = act_h.at[1 - j, span[h]]
            c_mj[h][1 - j] = net.send(src, act.at[1, c, 1 - j, span[h]], me.at_x(-1))

    def to_sibling(slot, h):
        part = act.at[slot, c, :, span[h]]
        c_s[h][slot] = net.send(part, part, me.sibling)

    def relay(h):
        c_pj[h][0].wait_recv()
        c_rp.append(net.send(act.at[3, c, 0, span[h]], act.at[2, c, 0, span[h]], me.at_x(1)))
        c_mj[h][1].wait_recv()
        c_rm.append(net.send(act.at[1, c, 1, span[h]], act.at[2, c, 1, span[h]], me.at_x(-1)))

    def near(h):
        c_pj[h][1].wait_recv()
        to_sibling(3, h)
        c_mj[h][0].wait_recv()
        to_sibling(1, h)

    def far(h):
        c_rp[h].wait_recv()
        c_rm[h].wait_recv()
        to_sibling(2, h)

    for h in range(2):
        c_sib.append(net.send(act_h.at[:, span[h]], act.at[0, c, :, span[h]], me.sibling))
    to_neighbours(0)
    c_tab = [net.send(tab.at[gy], tab.at[gy], me.at_gy(step)) for step in range(1, 8)]

    gain = gain_ref[...].astype(F32).reshape(1, 512)

    def prep(slot, core, h):
        for j in range(2):
            wide = act[slot, core, j, span[h], :].astype(F32)
            scaled[slot, h, 2 * core + j] = (wide * gain).astype(BF)
            square = wide * wide
            fold = (square[:, 0:128] + square[:, 128:256]) + (square[:, 256:384] + square[:, 384:512])
            row = jnp.sum(jnp.transpose(fold), axis=0, keepdims=True)
            sqall[h, 2 * core + j, pl.ds(wrap(x + slot), 1), pl.ds(0, 64)] = row

    def get_b(slot, h):
        def get(role):
            return prod[h, slot, wrap(y + role)]
        return get

    def role_z(slot):
        return wrap(x + slot - z + 4)

    def slot_z(role):
        return wrap(z + role - x + 4)

    ring_b = [
        [RingSum(net, get_b(k, h), yp, ym, bufs_b[h], k, 64) for k in range(4)] for h in range(2)
    ]
    sum_a = [BlockSum(net, role_z, slot_z, zp, zm, bufs_a[h], 4, 64) for h in range(2)]
    sum_b = [
        DirectSum(
            net, [out_b.at[h, slot_z(r)] for r in (1, 2, 3)], [me.at_z(r) for r in (1, 2, 3)],
            in_b.at[h],
        )
        for h in range(2)
    ]
    sum_a2 = [
        DirectSum(
            net, [out_a2.at[h, r - 1] for r in (1, 2, 3)], [me.at_y(r) for r in (1, 2, 3)],
            in_a2.at[h],
        )
        for h in range(2)
    ]

    def multiply_in(k, h):
        rows = scaled[k, h].reshape(256, 512)
        term = jnp.dot(rows, w[:, COLS:], preferred_element_type=F32)
        for j in range(4):
            prod[h, k, j] = term[j * 64 : (j + 1) * 64]
        ring_b[h][k].start_far()
        term = jnp.dot(rows, w[:, :COLS], preferred_element_type=F32).astype(BF)
        for j in range(4):
            sum_a[h].out[k, wrap(j - y)] = term[j * 64 : (j + 1) * 64]
        sum_a[h].block(k)
        ring_b[h][k].start_near()

    def block_b(slot, h):
        value = ring_b[h][slot].finish()
        keep_b[h, slot] = value
        out_b[h, slot] = value.astype(BF)
        for r in (1, 2, 3):

            @pl.when(role_z(slot) == r)
            def _():
                sum_b[h].copies[r - 1].start()

    def part_a2(h):
        for r in (2, 1, 3):
            out_a2[h, r - 1] = sum_a[h].finish(r).astype(BF)
            sum_a2[h].copies[r - 1].start()

    own_in.wait()
    prep(0, c, 0)
    for copy in w_in:
        copy.wait()
    c_sib[0].wait_recv()
    prep(0, 1 - c, 0)
    multiply_in(0, 0)
    relay(0)
    to_neighbours(1)
    prep(0, c, 1)
    c_sib[1].wait_recv()
    prep(0, 1 - c, 1)
    multiply_in(0, 1)
    near(0)
    ring_b[0][0].mid()
    prep(3, c, 0)
    prep(1, c, 0)
    c_s[0][3].wait_recv()
    prep(3, 1 - c, 0)
    multiply_in(3, 0)
    c_s[0][1].wait_recv()
    prep(1, 1 - c, 0)
    multiply_in(1, 0)
    far(0)
    relay(1)
    prep(2, c, 0)
    c_s[0][2].wait_recv()
    prep(2, 1 - c, 0)
    multiply_in(2, 0)
    near(1)
    sum_a[0].mid(0)
    ring_b[1][0].mid()
    ring_b[0][3].mid()
    ring_b[0][1].mid()
    block_b(0, 0)
    prep(3, c, 1)
    prep(1, c, 1)
    c_s[1][3].wait_recv()
    prep(3, 1 - c, 1)
    multiply_in(3, 1)
    far(1)
    c_s[1][1].wait_recv()
    prep(1, 1 - c, 1)
    multiply_in(1, 1)
    sum_a[0].mid(3)
    sum_a[0].mid(1)
    ring_b[0][2].mid()
    prep(2, c, 1)
    c_s[1][2].wait_recv()
    prep(2, 1 - c, 1)
    multiply_in(2, 1)
    k_in, v_in = fetch(k_h.at[0], kv), fetch(v_h.at[0], vv)
    wo_in = fetch(wo_h, wo)
    sq1 = [
        net.send(sqall.at[:, wrap(y + step)], sqr1.at[step - 1], me.at_y(step))
        for step in range(1, 4)
    ]
    block_b(3, 0)
    block_b(1, 0)
    sum_a[0].mid(2)
    sum_a[1].mid(0)
    block_b(0, 1)
    ring_b[1][3].mid()
    ring_b[1][1].mid()
    block_b(2, 0)
    sum_a[1].mid(3)
    sum_a[1].mid(1)
    ring_b[1][2].mid()
    for copy in sq1:
        copy.wait_recv()
    sqs[...] = (sqall[:, y] + sqr1[0]) + (sqr1[1] + sqr1[2])
    sq2 = [net.send(sqs, sqr2.at[step - 1], me.at_z(step)) for step in range(1, 4)]
    part_a2(0)
    sum_a[1].mid(2)
    block_b(3, 1)
    block_b(1, 1)
    block_b(2, 1)
    part_a2(1)
    for copy in sq2:
        copy.wait_recv()
    sqr1[0] = (sqs[...] + sqr2[0]) + (sqr2[1] + sqr2[2])
    halves = [
        jnp.transpose(
            jnp.broadcast_to(lax.rsqrt(sqr1[0, h, pl.ds(z, 1), :] / D + 1e-05), (128, 128))
        )[:64]
        for h in range(2)
    ]
    for copy in c_tab:
        copy.wait_recv()
    inverse = jnp.concatenate(halves, axis=0)
    both = tab[...].reshape(128, 128)
    turned = pltpu.roll(both, 64, 1)
    first = lax.broadcasted_iota(jnp.int32, (128, 128), 1) < 64
    cosine = jnp.where(first, both, turned)
    sine = jnp.where(first, -turned, both)
    slots = lax.broadcasted_iota(jnp.int32, (8, CTX), 1)
    bias[...] = jnp.where(slots < len_ref[0], 0.0, -1e30)

    def put(part, col, block):
        sendq[part, :, :, pl.ds(col, 128)] = block.astype(BF).reshape(8, 16, 128)

    def rotated(block):
        block = block * inverse
        return block * cosine + pltpu.roll(block, 64, 1) * sine

    partners = []
    for xx, cc in (
        (x, 1 - c),
        (x + 1 - 2 * lax.rem(x, 2), c),
        (x + 1 - 2 * lax.rem(x, 2), 1 - c),
        (wrap(x + 2), c),
        (wrap(x + 2), 1 - c),
        (3 - x, c),
        (3 - x, 1 - c),
    ):
        partners.append(xx * 2 + cc)

    def pass_on(part):
        recvq[part, gy] = sendq[part, gy]
        return [
            net.send(sendq.at[part, other], recvq.at[part, gy], (me.gx, other))
            for other in partners
        ]

    fin = jnp.concatenate([sum_b[h].finish(keep_b[h, slot_z(0)]) for h in range(2)], axis=0)
    for head in range(4):
        put(1, head * 128, rotated(fin[:, head * 128 : (head + 1) * 128]))
    put(1, 512, fin[:, 512:640] * inverse)
    pass_b = pass_on(1)
    fin = jnp.concatenate([sum_a2[h].finish(sum_a[h].finish(0)) for h in range(2)], axis=0)
    for head in range(5):
        put(0, head * 128, rotated(fin[:, head * 128 : (head + 1) * 128]))
    pass_a = pass_on(0)

    scale = HD ** (-0.5) * 1.4426950408889634
    contract = (((1,), (1,)), ((), ()))
    draft = lax.rem(lax.broadcasted_iota(jnp.int32, (128, 16), 0), 16)
    causal = lax.broadcasted_iota(jnp.int32, (128, 16), 1) <= draft
    home = g.at[lax.div(gy, 4), lax.rem(x, 2), 0, 0, pl.ds(pl.multiple_of(c * 16, 16), 16)]
    k_in.wait()
    v_in.wait()

    def attend(group):
        left, right = recvq[0, group], recvq[1, group]
        query = jnp.concatenate(
            [left[:, h * 128 : (h + 1) * 128] for h in range(4)]
            + [right[:, h * 128 : (h + 1) * 128] for h in range(4)],
            axis=0,
        )
        lanes = pl.ds(pl.multiple_of(group * 128, 128), 128)
        new = lax.dot_general(query, left[:, 512:640], contract, preferred_element_type=F32)
        new = jnp.where(causal, new, -1e30)
        peak = jnp.full((128, CHUNK), -1e30, F32)
        for at in range(0, CTX, CHUNK):
            old = lax.dot_general(
                query, kv[pl.ds(at, CHUNK), lanes], contract, preferred_element_type=F32
            )
            old = (old.reshape(16, 8, CHUNK) + bias[:, pl.ds(at, CHUNK)]).reshape(128, CHUNK)
            score[:, pl.ds(at, CHUNK)] = old
            peak = jnp.maximum(peak, old)
        highest = jnp.maximum(
            jnp.max(peak, axis=1, keepdims=True), jnp.max(new, axis=1, keepdims=True)
        )
        new = jnp.exp2((new - highest) * scale)
        blend = jnp.dot(new.astype(BF), right[:, 512:640], preferred_element_type=F32)
        sums = jnp.zeros((128, CHUNK), F32)
        for at in range(0, CTX, CHUNK):
            old = jnp.exp2((score[:, pl.ds(at, CHUNK)] - highest) * scale)
            sums = sums + old
            blend = blend + jnp.dot(
                old.astype(BF), vv[pl.ds(at, CHUNK), lanes], preferred_element_type=F32
            )
        total = jnp.sum(sums, axis=1, keepdims=True) + jnp.sum(new, axis=1, keepdims=True)
        result = (blend / total).astype(BF)
        return jnp.concatenate([result[h * 16 : (h + 1) * 16] for h in range(8)], axis=1)

    swap = []

    def attend_step(step):
        pass_a[step].wait_recv()
        pass_b[step].wait_recv()
        att[step] = attend(partners[step])
        swap.append(net.send(att.at[step], home, (me.gx, partners[step])))

    early = lax.div(x, 2)
    half_of = (early, 1 - early)
    rows_of_half = [pl.ds(pl.multiple_of(half * 64, 64), 64) for half in half_of]

    class Gather:
        def __init__(self, p):
            buf = g.at[half_of[p]]
            self.p = p
            self.a1 = RingCast(net, [buf.at[0, k, 0] for k in range(4)], zp, zm)
            self.b1 = RingCast(net, [buf.at[1, 0, k] for k in range(4)], yp, ym)
            self.a2 = [RingCast(net, [buf.at[0, j, k] for k in range(4)], yp, ym) for j in range(4)]
            self.b2 = [RingCast(net, [buf.at[1, k, j] for k in range(4)], zp, zm) for j in range(4)]

        def begin(self, copies):
            for copy in copies:
                copy.wait_recv()
            for ring in (self.a1, self.b1, self.a2[0], self.b2[0]):
                ring.start()

        def second(self):
            self.a1.relay()
            self.b1.relay()
            for ring in (self.a2[1], self.b2[1], self.a2[3], self.b2[3]):
                ring.start()

        def third(self):
            self.a2[0].relay()
            self.b2[0].relay()
            self.a1.far()
            self.b1.far()
            self.a2[2].start()
            self.b2[2].start()

        def fourth(self):
            for ring in (self.a2[1], self.b2[1], self.a2[3], self.b2[3]):
                ring.relay()

        def last(self):
            self.a2[2].relay()
            self.b2[2].relay()

        def complete(self, dy):
            self.b2[dy].far()
            if dy == 2:
                for ring in self.a2:
                    ring.far()

    mine = [lax.div(wrap(y + dy), 2) == c for dy in range(4)]
    pair = [
        [
            net.make(sib_send.at[dy, :, part], sib_recv.at[dy, :, part], me.sibling, False)
            for part in rows_of_half
        ]
        for dy in range(4)
    ]
    sum_x = [
        [
            [
                net.make(out_x.at[dy, r - 1, part], in_x.at[dy, r - 1, part], me.at_x(r), False)
                for r in (1, 2, 3)
            ]
            for part in rows_of_half
        ]
        for dy in range(4)
    ]

    def both_cores(dy, role, part):
        return sib_send[dy, role, part].astype(F32) + sib_recv[dy, role, part].astype(F32)

    def multiply(gather, dy):
        p = gather.p
        gather.complete(dy)
        rows = jnp.concatenate(
            [
                g[half_of[p], way, wrap(x + role - z + 4), dy]
                for role in range(4)
                for way in range(2)
            ],
            axis=0,
        )
        term = jnp.dot(rows, wo[...], preferred_element_type=F32).astype(BF)
        for role in range(4):
            sib_send[dy, role, rows_of_half[p], :] = term[role * 64 : (role + 1) * 64]

        @pl.when(jnp.logical_not(mine[dy]))
        def _():
            pair[dy][p].start()

    def sum_start(p, dy):
        @pl.when(mine[dy])
        def _():
            pair[dy][p].wait_recv()
            for r in (2, 1, 3):
                out_x[dy, r - 1, rows_of_half[p]] = both_cores(dy, r, rows_of_half[p]).astype(BF)
                sum_x[dy][p][r - 1].start()

    def sum_finish(dy):
        @pl.when(mine[dy])
        def _():
            base = lax.rem(wrap(y + dy), 2) * 128
            for copy in sum_x[dy][0] + sum_x[dy][1]:
                copy.wait_recv()
            for p in range(2):
                part = rows_of_half[p]
                total = both_cores(dy, 0, part)
                for r in range(3):
                    total = total + in_x[dy, r, part].astype(F32)
                rows = pl.ds(pl.multiple_of(base + half_of[p] * 64, 64), 64)
                out_ref[rows, :] = total.astype(BF)
                for copy in sum_x[dy][p]:
                    copy.wait_send()

        @pl.when(jnp.logical_not(mine[dy]))
        def _():
            for copy in pair[dy]:
                copy.wait_send()

    ge, gl = Gather(0), Gather(1)
    home[...] = attend(gy)
    for step in range(4):
        attend_step(step)
    ge.begin(swap[:3])
    attend_step(4)
    ge.second()
    attend_step(5)
    ge.third()
    attend_step(6)
    ge.fourth()
    gl.begin(swap[3:])
    ge.last()
    gl.second()
    wo_in.wait()
    multiply(ge, 0)
    gl.third()
    sum_start(0, 0)
    multiply(ge, 1)
    multiply(ge, 3)
    sum_start(0, 1)
    sum_start(0, 3)
    multiply(ge, 2)
    gl.fourth()
    sum_start(0, 2)
    multiply(gl, 0)
    gl.last()
    sum_start(1, 0)
    multiply(gl, 1)
    sum_start(1, 1)
    multiply(gl, 3)
    sum_start(1, 3)
    multiply(gl, 2)
    sum_start(1, 2)
    for dy in (0, 1, 3, 2):
        sum_finish(dy)
    net.drain()
    assert net.count == COPIES, net.count
    assert len(local) == 8


def layer(act, gain, wq, wk, wv, wo, freq, positions, lengths, key_cache, value_cache):
    hbm = pl.BlockSpec(memory_space=pl.ANY)
    vmem = pl.BlockSpec(memory_space=pltpu.VMEM)
    smem = pl.BlockSpec(memory_space=pltpu.SMEM)
    return pl.pallas_call(
        layer_kernel,
        out_shape=jax.ShapeDtypeStruct((256, 512), BF),
        in_specs=[hbm, vmem, hbm, hbm, hbm, hbm, vmem, smem, smem, hbm, hbm],
        out_specs=vmem,
        scratch_shapes=[
            pltpu.VMEM((4, 2, 2, 128, 512), BF),
            pltpu.VMEM((4, 2, 4, 64, 512), BF),
            pltpu.VMEM((512, 1280), BF),
            pltpu.VMEM((2, 4, 4, 64, COLS), F32),
            pltpu.VMEM((8, 16, 128), F32),
            pltpu.VMEM((2, 4, 8, 128), F32),
            pltpu.VMEM((3, 2, 8, 128), F32),
            pltpu.VMEM((2, 8, 128), F32),
            pltpu.VMEM((3, 2, 8, 128), F32),
            pltpu.VMEM((2, 8, 16, COLS), BF),
            pltpu.VMEM((2, 8, 16, COLS), BF),
            pltpu.VMEM((CTX, 1024), BF),
            pltpu.VMEM((CTX, 1024), BF),
            pltpu.VMEM((8, CTX), F32),
            pltpu.VMEM((128, CTX), F32),
            pltpu.VMEM((7, 16, 1024), BF),
            pltpu.VMEM((2, 2, 4, 4, 32, 1024), BF),
            pltpu.VMEM((1024, 512), BF),
            pltpu.VMEM((4, 4, 128, 512), BF),
            pltpu.VMEM((4, 4, 128, 512), BF),
            pltpu.VMEM((2, 4, 64, COLS), F32),
            *block_scratch(4, 64, COLS),
            *block_scratch(4, 64, COLS),
            *ring_scratch(4, 64, COLS),
            *ring_scratch(4, 64, COLS),
            pltpu.VMEM((2, 4, 64, COLS), BF),
            pltpu.VMEM((2, 3, 64, COLS), BF),
            pltpu.VMEM((2, 3, 64, COLS), BF),
            pltpu.VMEM((2, 3, 64, COLS), BF),
            pltpu.VMEM((4, 3, 128, 512), BF),
            pltpu.VMEM((4, 3, 128, 512), BF),
            pltpu.SemaphoreType.DMA((COPIES,)),
            pltpu.SemaphoreType.DMA((COPIES,)),
            pltpu.SemaphoreType.DMA((8,)),
        ],
        compiler_params=pltpu.CompilerParams(
            collective_id=0, has_side_effects=True, vmem_limit_bytes=60 * 1024 * 1024
        ),
        name="layer",
    )(act, gain, wq, wk, wv, wo, freq, positions, lengths, key_cache, value_cache)


def frequencies():
    power = np.arange(64, dtype=np.float64) * (-2.0 / HD)
    row = np.tile(np.power(500000.0, power), 2)
    return jnp.asarray(np.broadcast_to(row, (DRAFT, HD)).astype(np.float32))


def shards(act, gain, wq, wk, wv, wo, key_cache, value_cache, lengths, positions):
    out = layer(
        act.reshape(2, 128, 512), gain, wq, wk, wv, wo,
        frequencies(), positions, lengths, key_cache, value_cache,
    )
    return out.reshape(16, DRAFT, 512)


def solution(mesh):
    return jax.shard_map(
        shards,
        mesh=mesh,
        in_specs=(
            P("gy", None, "gx"),
            P("gx"),
            P("gx", "gy"),
            P("gx", "gy"),
            P("gx", "gy"),
            P("gy", "gx"),
            P(("gx", "gy"), None, None),
            P(("gx", "gy"), None, None),
            P(("gx", "gy")),
            P(("gx", "gy")),
        ),
        out_specs=P("gy", None, "gx"),
        check_vma=False,
    )
```

```python
import jax
import jax.numpy as jnp
import numpy as np
from jax import lax
from jax.experimental import pallas as pl
from jax.experimental.pallas import tpu as pltpu
from jax.sharding import PartitionSpec as P

D = 8192
HD = 128
KV = 8
CTX = 4096
DRAFT = 16
MESH = pl.DeviceIdType.MESH
F32 = jnp.float32
BF = jnp.bfloat16


def wrap(value, size=4):
    return lax.rem(value + size, size)


class Place:
    def __init__(self):
        gx, gy = lax.axis_index("gx"), lax.axis_index("gy")
        self.gx, self.gy = gx, gy
        self.z, self.y = lax.div(gx, 4), lax.rem(gx, 4)
        self.x, self.c = lax.div(gy, 2), lax.rem(gy, 2)
        self.sibling = (gx, gy + 1 - 2 * self.c)

    def at_x(self, step):
        return (self.gx, wrap(self.x + step) * 2 + self.c)

    def at_y(self, step):
        return (self.z * 4 + wrap(self.y + step), self.gy)

    def at_z(self, step):
        return (wrap(self.z + step) * 4 + self.y, self.gy)

    def at_gy(self, step):
        return (self.gx, wrap(self.gy + step, 8))


class Net:
    def __init__(self, send_sem, recv_sem):
        self.send_sem, self.recv_sem = send_sem, recv_sem
        self.count = 0
        self.sent = []

    def make(self, src, dst, device, drained=True):
        copy = pltpu.make_async_remote_copy(
            src_ref=src,
            dst_ref=dst,
            send_sem=self.send_sem.at[self.count],
            recv_sem=self.recv_sem.at[self.count],
            device_id=device,
            device_id_type=MESH,
        )
        self.count += 1
        if drained:
            self.sent.append(copy)
        return copy

    def send(self, src, dst, device):
        copy = self.make(src, dst, device)
        copy.start()
        return copy

    def drain(self):
        for copy in self.sent:
            copy.wait_send()


def greet(devices):
    barrier = pltpu.get_barrier_semaphore()
    for device in devices:
        pl.semaphore_signal(barrier, inc=1, device_id=device, device_id_type=MESH)
    pl.semaphore_wait(barrier, len(devices))


class RingSum:
    def __init__(self, net, get, plus, minus, bufs, lead, rows, drained=True):
        self.get = get
        self.rows, self.half = rows, rows // 2
        self.so, self.sp, self.sm, self.rom, self.rop, self.rdm, self.rdp, self.kp, self.km = [
            buf.at[lead] for buf in bufs
        ]
        lo, hi = pl.ds(0, self.half), pl.ds(self.half, self.half)
        self.lo, self.hi = lo, hi
        self.om = net.make(self.so.at[lo], self.rom, plus, drained)
        self.op = net.make(self.so.at[hi], self.rop, minus, drained)
        self.m1 = net.make(self.sp.at[hi], self.rdm.at[hi], plus, drained)
        self.p1 = net.make(self.sm.at[lo], self.rdp.at[lo], minus, drained)
        self.m2 = net.make(self.sp.at[lo], self.rdm.at[lo], plus, drained)
        self.p2 = net.make(self.sm.at[hi], self.rdp.at[hi], minus, drained)
        self.copies = [self.om, self.op, self.m1, self.p1, self.m2, self.p2]

    def start_far(self):
        self.so[...] = self.get(2).astype(BF)
        self.om.start()
        self.op.start()

    def start_near(self):
        h = self.half
        part = self.get(1)
        self.kp[...] = part[:h]
        self.sp[self.hi] = part[h:].astype(BF)
        self.m1.start()
        part = self.get(3)
        self.km[...] = part[h:]
        self.sm[self.lo] = part[:h].astype(BF)
        self.p1.start()

    def mid(self):
        self.om.wait_recv()
        self.sp[self.lo] = (self.kp[...] + self.rom[...].astype(F32)).astype(BF)
        self.m2.start()
        self.op.wait_recv()
        self.sm[self.hi] = (self.km[...] + self.rop[...].astype(F32)).astype(BF)
        self.p2.start()

    def finish(self):
        own = self.get(0)
        for copy in (self.m1, self.p1, self.m2, self.p2):
            copy.wait_recv()
        return own + self.rdm[...].astype(F32) + self.rdp[...].astype(F32)


class DirectSum:
    def __init__(self, net, sources, devices, landing, drained=True):
        self.landing = landing
        self.copies = [
            net.make(src, landing.at[i], device, drained)
            for i, (src, device) in enumerate(zip(sources, devices))
        ]

    def finish(self, own):
        for copy in self.copies:
            copy.wait_recv()
        a, b, c = (self.landing[i].astype(F32) for i in range(3))
        return (own + a) + (b + c)


def ring_scratch(count, rows, cols):
    h = rows // 2
    return [
        pltpu.VMEM((count, rows, cols), BF),
        pltpu.VMEM((count, rows, cols), BF),
        pltpu.VMEM((count, rows, cols), BF),
        pltpu.VMEM((count, h, cols), BF),
        pltpu.VMEM((count, h, cols), BF),
        pltpu.VMEM((count, rows, cols), BF),
        pltpu.VMEM((count, rows, cols), BF),
        pltpu.VMEM((count, h, cols), F32),
        pltpu.VMEM((count, h, cols), F32),
    ]


class BlockSum:
    def __init__(self, net, role, slot, plus, minus, bufs, parts, rows):
        self.role, self.slot, self.parts = role, slot, parts
        self.out, self.rom, self.rop, self.rdm, self.rdp = bufs
        h = rows // 2
        lo, hi = pl.ds(0, h), pl.ds(h, h)
        self.lo, self.hi = lo, hi
        far, near, last = slot(2), slot(1), slot(3)
        span = range(parts)
        self.om = [net.make(self.out.at[far, j, lo], self.rom.at[j], plus) for j in span]
        self.op = [net.make(self.out.at[far, j, hi], self.rop.at[j], minus) for j in span]
        self.m1 = [net.make(self.out.at[near, j, hi], self.rdm.at[j, hi], plus) for j in span]
        self.p1 = [net.make(self.out.at[last, j, lo], self.rdp.at[j, lo], minus) for j in span]
        self.m2 = [net.make(self.out.at[near, j, lo], self.rdm.at[j, lo], plus) for j in span]
        self.p2 = [net.make(self.out.at[last, j, hi], self.rdp.at[j, hi], minus) for j in span]

    def block(self, k):
        role = self.role(k)

        @pl.when(role == 2)
        def _():
            for j in (2, 1, 3, 0):
                self.om[j].start()
                self.op[j].start()

        @pl.when(role == 1)
        def _():
            for j in (2, 1, 3, 0):
                self.m1[j].start()

        @pl.when(role == 3)
        def _():
            for j in (2, 1, 3, 0):
                self.p1[j].start()

    def value(self, k, j, rows):
        return self.out[k, j, rows].astype(F32)

    def mid(self, k):
        role = self.role(k)
        order = (2, 1, 3, 0)

        @pl.when(role == 1)
        def _():
            for j in order:
                self.om[j].wait_recv()
                total = self.value(k, j, self.lo) + self.rom[j].astype(F32)
                self.out[k, j, self.lo] = total.astype(BF)
                self.m2[j].start()

        @pl.when(role == 3)
        def _():
            for j in order:
                self.op[j].wait_recv()
                total = self.value(k, j, self.hi) + self.rop[j].astype(F32)
                self.out[k, j, self.hi] = total.astype(BF)
                self.p2[j].start()

    def finish(self, j):
        own = self.value(self.slot(0), j, slice(None))
        for copy in (self.m1[j], self.p1[j], self.m2[j], self.p2[j]):
            copy.wait_recv()
        return own + self.rdm[j].astype(F32) + self.rdp[j].astype(F32)


def block_scratch(parts, rows, cols):
    return [
        pltpu.VMEM((4, parts, rows, cols), BF),
        pltpu.VMEM((parts, rows // 2, cols), BF),
        pltpu.VMEM((parts, rows // 2, cols), BF),
        pltpu.VMEM((parts, rows, cols), BF),
        pltpu.VMEM((parts, rows, cols), BF),
    ]


class RingCast:
    def __init__(self, net, slots, plus, minus):
        lo, hi = pl.ds(0, 16), pl.ds(16, 16)
        own, next_, far, last = slots
        self.to_plus = net.make(own, last, plus)
        self.to_minus = net.make(own, next_, minus)
        self.on_plus = net.make(last.at[lo], far.at[lo], plus)
        self.on_minus = net.make(next_.at[hi], far.at[hi], minus)

    def start(self):
        self.to_plus.start()
        self.to_minus.start()

    def relay(self):
        self.to_plus.wait_recv()
        self.on_plus.start()
        self.to_minus.wait_recv()
        self.on_minus.start()

    def far(self):
        self.on_plus.wait_recv()
        self.on_minus.wait_recv()


COLS = 640
COPIES = 274
CHUNK = 1024


def layer_kernel(
    act_h, gain_ref, wq_h, wk_h, wv_h, wo_h, freq_ref, pos_ref, len_ref, k_h, v_h, out_ref,
    act, scaled, w, prod, tab, sqall, sqr1, sqs, sqr2, sendq, recvq, kv, vv, bias, score, att,
    g, wo, sib_send, sib_recv, keep_b, *rest,
):
    bufs_a = [rest[:5], rest[5:10]]
    bufs_b = [rest[10:19], rest[19:28]]
    out_b, in_b, out_a2, in_a2, out_x, in_x, send_sem, recv_sem, local_sem = rest[28:]
    me = Place()
    x, c, y, z, gy = me.x, me.c, me.y, me.z, me.gy
    net = Net(send_sem, recv_sem)
    ym, yp, zm, zp = me.at_y(-1), me.at_y(1), me.at_z(-1), me.at_z(1)

    local = []

    def fetch(src, dst):
        copy = pltpu.make_async_copy(src, dst, local_sem.at[len(local)])
        copy.start()
        local.append(copy)
        return copy

    own_in = fetch(act_h, act.at[0, c])
    w_in = [
        fetch(wq_h.at[:, pl.ds(0, 512)], w.at[:, pl.ds(0, 512)]),
        fetch(wk_h, w.at[:, pl.ds(512, 128)]),
        fetch(wq_h.at[:, pl.ds(512, 512)], w.at[:, pl.ds(640, 512)]),
        fetch(wv_h, w.at[:, pl.ds(1152, 128)]),
    ]
    token = lax.broadcasted_iota(jnp.int32, (DRAFT, HD), 0)
    angles = (pos_ref[0] + token).astype(F32) * freq_ref[...]
    half = lax.broadcasted_iota(jnp.int32, (DRAFT, HD), 1) < HD // 2
    tab[gy] = jnp.where(half, jnp.cos(angles), jnp.sin(angles))

    greet(
        [me.at_gy(step) for step in range(1, 8)]
        + [me.at_y(step) for step in range(1, 4)]
        + [me.at_z(step) for step in range(1, 4)]
    )

    span = (pl.ds(0, 64), pl.ds(64, 64))
    c_sib, c_pj, c_mj, c_rp, c_rm, c_s = [], [], [], [], [], [{}, {}]

    def to_neighbours(h):
        c_pj.append([None, None])
        c_mj.append([None, None])
        for j in range(2):
            src = act_h.at[j, span[h]]
            c_pj[h][j] = net.send(src, act.at[3, c, j, span[h]], me.at_x(1))
            src = act_h.at[1 - j, span[h]]
            c_mj[h][1 - j] = net.send(src, act.at[1, c, 1 - j, span[h]], me.at_x(-1))

    def to_sibling(slot, h):
        part = act.at[slot, c, :, span[h]]
        c_s[h][slot] = net.send(part, part, me.sibling)

    def relay(h):
        c_pj[h][0].wait_recv()
        c_rp.append(net.send(act.at[3, c, 0, span[h]], act.at[2, c, 0, span[h]], me.at_x(1)))
        c_mj[h][1].wait_recv()
        c_rm.append(net.send(act.at[1, c, 1, span[h]], act.at[2, c, 1, span[h]], me.at_x(-1)))

    def near(h):
        c_pj[h][1].wait_recv()
        to_sibling(3, h)
        c_mj[h][0].wait_recv()
        to_sibling(1, h)

    def far(h):
        c_rp[h].wait_recv()
        c_rm[h].wait_recv()
        to_sibling(2, h)

    for h in range(2):
        c_sib.append(net.send(act_h.at[:, span[h]], act.at[0, c, :, span[h]], me.sibling))
    to_neighbours(0)
    c_tab = [net.send(tab.at[gy], tab.at[gy], me.at_gy(step)) for step in range(1, 8)]

    gain = gain_ref[...].astype(F32).reshape(1, 512)

    def prep(slot, core, h):
        for j in range(2):
            wide = act[slot, core, j, span[h], :].astype(F32)
            scaled[slot, h, 2 * core + j] = (wide * gain).astype(BF)
            square = wide * wide
            fold = (square[:, 0:128] + square[:, 128:256]) + (square[:, 256:384] + square[:, 384:512])
            row = jnp.sum(jnp.transpose(fold), axis=0, keepdims=True)
            sqall[h, 2 * core + j, pl.ds(wrap(x + slot), 1), pl.ds(0, 64)] = row

    def get_b(slot, h):
        def get(role):
            return prod[h, slot, wrap(y + role)]
        return get

    def role_z(slot):
        return wrap(x + slot - z + 4)

    def slot_z(role):
        return wrap(z + role - x + 4)

    ring_b = [
        [RingSum(net, get_b(k, h), yp, ym, bufs_b[h], k, 64) for k in range(4)] for h in range(2)
    ]
    sum_a = [BlockSum(net, role_z, slot_z, zp, zm, bufs_a[h], 4, 64) for h in range(2)]
    sum_b = [
        DirectSum(
            net, [out_b.at[h, slot_z(r)] for r in (1, 2, 3)], [me.at_z(r) for r in (1, 2, 3)],
            in_b.at[h],
        )
        for h in range(2)
    ]
    sum_a2 = [
        DirectSum(
            net, [out_a2.at[h, r - 1] for r in (1, 2, 3)], [me.at_y(r) for r in (1, 2, 3)],
            in_a2.at[h],
        )
        for h in range(2)
    ]

    def multiply_in(k, h):
        rows = scaled[k, h].reshape(256, 512)
        term = jnp.dot(rows, w[:, :COLS], preferred_element_type=F32).astype(BF)
        for j in range(4):
            sum_a[h].out[k, wrap(j - y)] = term[j * 64 : (j + 1) * 64]
        sum_a[h].block(k)
        term = jnp.dot(rows, w[:, COLS:], preferred_element_type=F32)
        for j in range(4):
            prod[h, k, j] = term[j * 64 : (j + 1) * 64]
        ring_b[h][k].start_far()
        ring_b[h][k].start_near()

    def block_b(slot, h):
        value = ring_b[h][slot].finish()
        keep_b[h, slot] = value
        out_b[h, slot] = value.astype(BF)
        for r in (1, 2, 3):

            @pl.when(role_z(slot) == r)
            def _():
                sum_b[h].copies[r - 1].start()

    def part_a2(h):
        for r in (2, 1, 3):
            out_a2[h, r - 1] = sum_a[h].finish(r).astype(BF)
            sum_a2[h].copies[r - 1].start()

    own_in.wait()
    prep(0, c, 0)
    for copy in w_in:
        copy.wait()
    c_sib[0].wait_recv()
    prep(0, 1 - c, 0)
    multiply_in(0, 0)
    relay(0)
    to_neighbours(1)
    prep(0, c, 1)
    c_sib[1].wait_recv()
    prep(0, 1 - c, 1)
    multiply_in(0, 1)
    near(0)
    ring_b[0][0].mid()
    prep(3, c, 0)
    prep(1, c, 0)
    c_s[0][3].wait_recv()
    prep(3, 1 - c, 0)
    multiply_in(3, 0)
    c_s[0][1].wait_recv()
    prep(1, 1 - c, 0)
    multiply_in(1, 0)
    far(0)
    relay(1)
    prep(2, c, 0)
    c_s[0][2].wait_recv()
    prep(2, 1 - c, 0)
    multiply_in(2, 0)
    near(1)
    sum_a[0].mid(0)
    ring_b[1][0].mid()
    ring_b[0][3].mid()
    ring_b[0][1].mid()
    block_b(0, 0)
    prep(3, c, 1)
    prep(1, c, 1)
    c_s[1][3].wait_recv()
    prep(3, 1 - c, 1)
    multiply_in(3, 1)
    far(1)
    c_s[1][1].wait_recv()
    prep(1, 1 - c, 1)
    multiply_in(1, 1)
    sum_a[0].mid(3)
    sum_a[0].mid(1)
    ring_b[0][2].mid()
    prep(2, c, 1)
    c_s[1][2].wait_recv()
    prep(2, 1 - c, 1)
    multiply_in(2, 1)
    k_in, v_in = fetch(k_h.at[0], kv), fetch(v_h.at[0], vv)
    wo_in = fetch(wo_h, wo)
    sq1 = [
        net.send(sqall.at[:, wrap(y + step)], sqr1.at[step - 1], me.at_y(step))
        for step in range(1, 4)
    ]
    block_b(3, 0)
    block_b(1, 0)
    sum_a[0].mid(2)
    sum_a[1].mid(0)
    block_b(0, 1)
    ring_b[1][3].mid()
    ring_b[1][1].mid()
    block_b(2, 0)
    sum_a[1].mid(3)
    sum_a[1].mid(1)
    ring_b[1][2].mid()
    for copy in sq1:
        copy.wait_recv()
    sqs[...] = (sqall[:, y] + sqr1[0]) + (sqr1[1] + sqr1[2])
    sq2 = [net.send(sqs, sqr2.at[step - 1], me.at_z(step)) for step in range(1, 4)]
    part_a2(0)
    sum_a[1].mid(2)
    block_b(3, 1)
    block_b(1, 1)
    block_b(2, 1)
    part_a2(1)
    for copy in sq2:
        copy.wait_recv()
    sqr1[0] = (sqs[...] + sqr2[0]) + (sqr2[1] + sqr2[2])
    halves = [
        jnp.transpose(
            jnp.broadcast_to(lax.rsqrt(sqr1[0, h, pl.ds(z, 1), :] / D + 1e-05), (128, 128))
        )[:64]
        for h in range(2)
    ]
    for copy in c_tab:
        copy.wait_recv()
    inverse = jnp.concatenate(halves, axis=0)
    both = tab[...].reshape(128, 128)
    turned = pltpu.roll(both, 64, 1)
    first = lax.broadcasted_iota(jnp.int32, (128, 128), 1) < 64
    cosine = jnp.where(first, both, turned)
    sine = jnp.where(first, -turned, both)
    slots = lax.broadcasted_iota(jnp.int32, (8, CTX), 1)
    bias[...] = jnp.where(slots < len_ref[0], 0.0, -1e30)

    def put(part, col, block):
        sendq[part, :, :, pl.ds(col, 128)] = block.astype(BF).reshape(8, 16, 128)

    def rotated(block):
        block = block * inverse
        return block * cosine + pltpu.roll(block, 64, 1) * sine

    partners = []
    for xx, cc in (
        (x, 1 - c),
        (x + 1 - 2 * lax.rem(x, 2), c),
        (x + 1 - 2 * lax.rem(x, 2), 1 - c),
        (wrap(x + 2), c),
        (wrap(x + 2), 1 - c),
        (3 - x, c),
        (3 - x, 1 - c),
    ):
        partners.append(xx * 2 + cc)

    def pass_on(part):
        recvq[part, gy] = sendq[part, gy]
        return [
            net.send(sendq.at[part, other], recvq.at[part, gy], (me.gx, other))
            for other in partners
        ]

    fin = jnp.concatenate([sum_b[h].finish(keep_b[h, slot_z(0)]) for h in range(2)], axis=0)
    for head in range(4):
        put(1, head * 128, rotated(fin[:, head * 128 : (head + 1) * 128]))
    put(1, 512, fin[:, 512:640] * inverse)
    pass_b = pass_on(1)
    fin = jnp.concatenate([sum_a2[h].finish(sum_a[h].finish(0)) for h in range(2)], axis=0)
    for head in range(5):
        put(0, head * 128, rotated(fin[:, head * 128 : (head + 1) * 128]))
    pass_a = pass_on(0)

    scale = HD ** (-0.5) * 1.4426950408889634
    contract = (((1,), (1,)), ((), ()))
    draft = lax.rem(lax.broadcasted_iota(jnp.int32, (128, 16), 0), 16)
    causal = lax.broadcasted_iota(jnp.int32, (128, 16), 1) <= draft
    home = g.at[lax.div(gy, 4), lax.rem(x, 2), 0, 0, pl.ds(pl.multiple_of(c * 16, 16), 16)]
    k_in.wait()
    v_in.wait()

    def attend(group):
        left, right = recvq[0, group], recvq[1, group]
        query = jnp.concatenate(
            [left[:, h * 128 : (h + 1) * 128] for h in range(4)]
            + [right[:, h * 128 : (h + 1) * 128] for h in range(4)],
            axis=0,
        )
        lanes = pl.ds(pl.multiple_of(group * 128, 128), 128)
        new = lax.dot_general(query, left[:, 512:640], contract, preferred_element_type=F32)
        new = jnp.where(causal, new, -1e30)
        peak = jnp.full((128, CHUNK), -1e30, F32)
        for at in range(0, CTX, CHUNK):
            old = lax.dot_general(
                query, kv[pl.ds(at, CHUNK), lanes], contract, preferred_element_type=F32
            )
            old = (old.reshape(16, 8, CHUNK) + bias[:, pl.ds(at, CHUNK)]).reshape(128, CHUNK)
            score[:, pl.ds(at, CHUNK)] = old
            peak = jnp.maximum(peak, old)
        highest = jnp.maximum(
            jnp.max(peak, axis=1, keepdims=True), jnp.max(new, axis=1, keepdims=True)
        )
        new = jnp.exp2((new - highest) * scale)
        blend = jnp.dot(new.astype(BF), right[:, 512:640], preferred_element_type=F32)
        sums = jnp.zeros((128, CHUNK), F32)
        for at in range(0, CTX, CHUNK):
            old = jnp.exp2((score[:, pl.ds(at, CHUNK)] - highest) * scale)
            sums = sums + old
            blend = blend + jnp.dot(
                old.astype(BF), vv[pl.ds(at, CHUNK), lanes], preferred_element_type=F32
            )
        total = jnp.sum(sums, axis=1, keepdims=True) + jnp.sum(new, axis=1, keepdims=True)
        result = (blend / total).astype(BF)
        return jnp.concatenate([result[h * 16 : (h + 1) * 16] for h in range(8)], axis=1)

    swap = []

    def attend_step(step):
        pass_a[step].wait_recv()
        pass_b[step].wait_recv()
        att[step] = attend(partners[step])
        swap.append(net.send(att.at[step], home, (me.gx, partners[step])))

    early = lax.div(x, 2)
    half_of = (early, 1 - early)
    rows_of_half = [pl.ds(pl.multiple_of(half * 64, 64), 64) for half in half_of]

    class Gather:
        def __init__(self, p):
            buf = g.at[half_of[p]]
            self.p = p
            self.a1 = RingCast(net, [buf.at[0, k, 0] for k in range(4)], zp, zm)
            self.b1 = RingCast(net, [buf.at[1, 0, k] for k in range(4)], yp, ym)
            self.a2 = [RingCast(net, [buf.at[0, j, k] for k in range(4)], yp, ym) for j in range(4)]
            self.b2 = [RingCast(net, [buf.at[1, k, j] for k in range(4)], zp, zm) for j in range(4)]

        def begin(self, copies):
            for copy in copies:
                copy.wait_recv()
            for ring in (self.a1, self.b1, self.a2[0], self.b2[0]):
                ring.start()

        def second(self):
            self.a1.relay()
            self.b1.relay()
            for ring in (self.a2[1], self.b2[1], self.a2[3], self.b2[3]):
                ring.start()

        def third(self):
            self.a2[0].relay()
            self.b2[0].relay()
            self.a1.far()
            self.b1.far()
            self.a2[2].start()
            self.b2[2].start()

        def fourth(self):
            for ring in (self.a2[1], self.b2[1], self.a2[3], self.b2[3]):
                ring.relay()

        def last(self):
            self.a2[2].relay()
            self.b2[2].relay()

        def complete(self, dy):
            self.b2[dy].far()
            if dy == 2:
                for ring in self.a2:
                    ring.far()

    mine = [lax.div(wrap(y + dy), 2) == c for dy in range(4)]
    pair = [
        [
            net.make(sib_send.at[dy, :, part], sib_recv.at[dy, :, part], me.sibling, False)
            for part in rows_of_half
        ]
        for dy in range(4)
    ]
    sum_x = [
        [
            [
                net.make(out_x.at[dy, r - 1, part], in_x.at[dy, r - 1, part], me.at_x(r), False)
                for r in (1, 2, 3)
            ]
            for part in rows_of_half
        ]
        for dy in range(4)
    ]

    def both_cores(dy, role, part):
        return sib_send[dy, role, part].astype(F32) + sib_recv[dy, role, part].astype(F32)

    def multiply(gather, dy):
        p = gather.p
        gather.complete(dy)
        rows = jnp.concatenate(
            [
                g[half_of[p], way, wrap(x + role - z + 4), dy]
                for role in range(4)
                for way in range(2)
            ],
            axis=0,
        )
        term = jnp.dot(rows, wo[...], preferred_element_type=F32).astype(BF)
        for role in range(4):
            sib_send[dy, role, rows_of_half[p], :] = term[role * 64 : (role + 1) * 64]

        @pl.when(jnp.logical_not(mine[dy]))
        def _():
            pair[dy][p].start()

    def sum_start(p, dy):
        @pl.when(mine[dy])
        def _():
            pair[dy][p].wait_recv()
            for r in (2, 1, 3):
                out_x[dy, r - 1, rows_of_half[p]] = both_cores(dy, r, rows_of_half[p]).astype(BF)
                sum_x[dy][p][r - 1].start()

    def sum_finish(dy):
        @pl.when(mine[dy])
        def _():
            base = lax.rem(wrap(y + dy), 2) * 128
            for copy in sum_x[dy][0] + sum_x[dy][1]:
                copy.wait_recv()
            for p in range(2):
                part = rows_of_half[p]
                total = both_cores(dy, 0, part)
                for r in range(3):
                    total = total + in_x[dy, r, part].astype(F32)
                rows = pl.ds(pl.multiple_of(base + half_of[p] * 64, 64), 64)
                out_ref[rows, :] = total.astype(BF)
                for copy in sum_x[dy][p]:
                    copy.wait_send()

        @pl.when(jnp.logical_not(mine[dy]))
        def _():
            for copy in pair[dy]:
                copy.wait_send()

    ge, gl = Gather(0), Gather(1)
    home[...] = attend(gy)
    for step in range(4):
        attend_step(step)
    ge.begin(swap[:3])
    attend_step(4)
    ge.second()
    attend_step(5)
    ge.third()
    attend_step(6)
    ge.fourth()
    gl.begin(swap[3:])
    ge.last()
    gl.second()
    wo_in.wait()
    multiply(ge, 0)
    gl.third()
    sum_start(0, 0)
    multiply(ge, 1)
    multiply(ge, 3)
    sum_start(0, 1)
    sum_start(0, 3)
    multiply(ge, 2)
    gl.fourth()
    sum_start(0, 2)
    multiply(gl, 0)
    gl.last()
    sum_start(1, 0)
    multiply(gl, 1)
    sum_start(1, 1)
    multiply(gl, 3)
    sum_start(1, 3)
    multiply(gl, 2)
    sum_start(1, 2)
    for dy in (0, 1, 3, 2):
        sum_finish(dy)
    net.drain()
    assert net.count == COPIES, net.count
    assert len(local) == 8


def layer(act, gain, wq, wk, wv, wo, freq, positions, lengths, key_cache, value_cache):
    hbm = pl.BlockSpec(memory_space=pl.ANY)
    vmem = pl.BlockSpec(memory_space=pltpu.VMEM)
    smem = pl.BlockSpec(memory_space=pltpu.SMEM)
    return pl.pallas_call(
        layer_kernel,
        out_shape=jax.ShapeDtypeStruct((256, 512), BF),
        in_specs=[hbm, vmem, hbm, hbm, hbm, hbm, vmem, smem, smem, hbm, hbm],
        out_specs=vmem,
        scratch_shapes=[
            pltpu.VMEM((4, 2, 2, 128, 512), BF),
            pltpu.VMEM((4, 2, 4, 64, 512), BF),
            pltpu.VMEM((512, 1280), BF),
            pltpu.VMEM((2, 4, 4, 64, COLS), F32),
            pltpu.VMEM((8, 16, 128), F32),
            pltpu.VMEM((2, 4, 8, 128), F32),
            pltpu.VMEM((3, 2, 8, 128), F32),
            pltpu.VMEM((2, 8, 128), F32),
            pltpu.VMEM((3, 2, 8, 128), F32),
            pltpu.VMEM((2, 8, 16, COLS), BF),
            pltpu.VMEM((2, 8, 16, COLS), BF),
            pltpu.VMEM((CTX, 1024), BF),
            pltpu.VMEM((CTX, 1024), BF),
            pltpu.VMEM((8, CTX), F32),
            pltpu.VMEM((128, CTX), F32),
            pltpu.VMEM((7, 16, 1024), BF),
            pltpu.VMEM((2, 2, 4, 4, 32, 1024), BF),
            pltpu.VMEM((1024, 512), BF),
            pltpu.VMEM((4, 4, 128, 512), BF),
            pltpu.VMEM((4, 4, 128, 512), BF),
            pltpu.VMEM((2, 4, 64, COLS), F32),
            *block_scratch(4, 64, COLS),
            *block_scratch(4, 64, COLS),
            *ring_scratch(4, 64, COLS),
            *ring_scratch(4, 64, COLS),
            pltpu.VMEM((2, 4, 64, COLS), BF),
            pltpu.VMEM((2, 3, 64, COLS), BF),
            pltpu.VMEM((2, 3, 64, COLS), BF),
            pltpu.VMEM((2, 3, 64, COLS), BF),
            pltpu.VMEM((4, 3, 128, 512), BF),
            pltpu.VMEM((4, 3, 128, 512), BF),
            pltpu.SemaphoreType.DMA((COPIES,)),
            pltpu.SemaphoreType.DMA((COPIES,)),
            pltpu.SemaphoreType.DMA((8,)),
        ],
        compiler_params=pltpu.CompilerParams(
            collective_id=0, has_side_effects=True, vmem_limit_bytes=60 * 1024 * 1024
        ),
        name="layer",
    )(act, gain, wq, wk, wv, wo, freq, positions, lengths, key_cache, value_cache)


def frequencies():
    power = np.arange(64, dtype=np.float64) * (-2.0 / HD)
    row = np.tile(np.power(500000.0, power), 2)
    return jnp.asarray(np.broadcast_to(row, (DRAFT, HD)).astype(np.float32))


def shards(act, gain, wq, wk, wv, wo, key_cache, value_cache, lengths, positions):
    out = layer(
        act.reshape(2, 128, 512), gain, wq, wk, wv, wo,
        frequencies(), positions, lengths, key_cache, value_cache,
    )
    return out.reshape(16, DRAFT, 512)


def solution(mesh):
    return jax.shard_map(
        shards,
        mesh=mesh,
        in_specs=(
            P("gy", None, "gx"),
            P("gx"),
            P("gx", "gy"),
            P("gx", "gy"),
            P("gx", "gy"),
            P("gy", "gx"),
            P(("gx", "gy"), None, None),
            P(("gx", "gy"), None, None),
            P(("gx", "gy")),
            P(("gx", "gy")),
        ),
        out_specs=P("gy", None, "gx"),
        check_vma=False,
    )
```
